128 devices in a mesh: ctx: 64 (over y_lo, x, z, core), ch: 2 (over y_hi).
Axes of the slice: x: 4, y: 4 (y_hi: 2, y_lo: 2; y = y_hi * 2 + y_lo), z: 4, core: 2. Of those that a mesh axis runs over, the one named last changes fastest.
Arguments:
- tokens: bfloat16 [32768, 8192], P('ctx', 'ch'), may hold values from -6 to 6
- in_weight: bfloat16 [8192, 1024], P('ch'), may hold values from -0.0625 to 0.0625
- filter_taps: float32 [32768, 1024], P('ctx', 'ch'), may hold values from -0.03125 to 0.03125
- skip_gain: float32 [1024], P('ch'), may hold values from 0.25 to 1.75
- out_weight: bfloat16 [1024, 8192], P('ch'), may hold values from -0.1875 to 0.1875
Outputs:
- mixed: bfloat16 [32768, 8192], P('ctx', 'ch')
The draws below stay inside these ranges and needn't reach their ends.
All inputs are finite; a program needn't handle non-finite values.
Results may differ from the reference program's by a relative error of at most 0.0049.
Values may be sent and summed in bfloat16 or wider, within the bound.
No kernel may reach another device: no remote copies, remote signals or barrier semaphores. Data moves between devices by JAX's collectives and lax.ppermute only.
A program may use at most 128 MiB of HBM per device.

```python
import jax
import jax.numpy as jnp

D = 8192
C = 1024
SEQ = 32768


def block_scale(stream_key, dims, split, low, top_value):
    gain = 1.0
    for position, blocks in split:
        heights = jax.random.uniform(jax.random.fold_in(jax.random.fold_in(stream_key, 6), position), (blocks,), jnp.float32, low / len(split), top_value / len(split))
        gain = gain * jnp.repeat(jnp.exp(heights), dims[position] // blocks).reshape((-1,) + (1,) * (len(dims) - 1 - position))
    return gain


def bell_draw(key, dims, scale, bound, cuts=(), dtype=jnp.bfloat16):
    values = jax.random.normal(key, dims, jnp.float32) * scale
    if len(cuts) > 0:
        values = block_scale(key, dims, cuts, -0.22, 0.18) * values
    return jnp.clip(values, min=-bound, max=bound).astype(dtype)


def setup_inputs(seed: int = 0) -> dict:
    seeds = jax.random.split(jax.random.key(seed), 6)
    tokens = bell_draw(seeds[0], (SEQ, D), 1.0, 6.0, ((0, 64), (1, 2)))
    in_weight = bell_draw(seeds[1], (D, C), D ** -0.5, 0.0625, ((0, 2),))
    filter_taps = bell_draw(seeds[2], (SEQ, C), SEQ ** -0.5, 0.03125, ((0, 64), (1, 2)), jnp.float32)
    skip_gain = jnp.clip(0.25 + 1.5 * jax.random.uniform(seeds[3], (C,), jnp.float32) ** block_scale(seeds[3], (C,), ((0, 2),), -0.2, 0.2), 0.25, 1.75)
    out_weight = bell_draw(seeds[4], (C, D), C ** -0.5, 0.1875, ((0, 2),))
    return dict(tokens=tokens, in_weight=in_weight, filter_taps=filter_taps, skip_gain=skip_gain, out_weight=out_weight)


def reference(tokens, in_weight, filter_taps, skip_gain, out_weight):
    projected = jnp.dot(tokens, in_weight, preferred_element_type=jnp.float32)
    length = 2 * projected.shape[0]
    signal = jnp.fft.rfft(projected, n=length, axis=0)
    response = jnp.fft.rfft(filter_taps, n=length, axis=0)
    convolved = jnp.fft.irfft(signal * response, n=length, axis=0)[: projected.shape[0]]
    convolved = convolved.astype(jnp.float32)
    mixed_in = (convolved + skip_gain[None, :] * projected).astype(jnp.bfloat16)
    return jnp.dot(mixed_in, out_weight, preferred_element_type=jnp.float32).astype(jnp.bfloat16)
```

```python
import numpy as np
import ml_dtypes
import jax
import jax.numpy as jnp
from jax import lax
from jax.experimental import pallas as pl
from jax.experimental.pallas import tpu as pltpu
from jax.sharding import PartitionSpec as P

bf16 = jnp.bfloat16
f32 = jnp.float32
LINES = 72
MIB = 1024 * 1024


def split_table(table):
    high = table.astype(ml_dtypes.bfloat16)
    low = (table - high.astype(np.float64)).astype(ml_dtypes.bfloat16)
    return high, low


def tables(blocks, width):
    period = 2 * blocks * width
    half = width // 2
    freq = np.arange(LINES)[:, None]
    live = (freq <= blocks).astype(np.float64)
    angle = 2.0 * np.pi * (freq * np.arange(blocks)[None, :] % (2 * blocks)) / (2 * blocks)
    lead = np.concatenate([np.cos(angle) * live, -np.sin(angle) * live], axis=0)
    lead_high, lead_low = split_table(lead)
    lead_signal = np.concatenate([lead_high, lead_high, lead_low], axis=1)
    lead_taps = np.concatenate([lead_high, lead_low], axis=1)
    weight = np.where((freq == 0) | (freq == blocks), 1.0, 2.0) * live / period
    tail = np.concatenate([np.cos(angle) * weight, -np.sin(angle) * weight], axis=0).T
    tail_high, tail_low = split_table(tail)
    rows = 6 * LINES
    tail3 = np.concatenate(
        [tail_high, tail_high, tail_low, np.zeros((blocks, -rows % 256), ml_dtypes.bfloat16)], axis=1
    )
    turn = 2.0 * np.pi * freq * np.arange(width)[None, :] / period
    twist = np.stack([np.cos(turn), np.sin(turn)]).astype(np.float32)
    fold = 2.0 * np.pi * np.arange(half) / width
    fold = np.stack([np.cos(fold), np.sin(fold)]).astype(np.float32)
    index = np.arange(half)
    line = 2.0 * np.pi * (index[:, None] * index[None, :] % half) / half
    cos, sin = np.cos(line), np.sin(line)
    forward = np.block([[cos, -sin], [sin, cos]])
    forward_high, forward_low = split_table(forward)
    return dict(
        lead_signal=lead_signal,
        lead_taps=lead_taps,
        tail=tail3,
        twist=twist,
        fold=fold,
        forward=np.stack([forward_high, forward_low]),
        backward=np.stack([forward_high.T, forward_low.T]),
    )


def dot(a, b):
    return jnp.dot(a, b, preferred_element_type=f32)


def split(a):
    high = a.astype(bf16)
    return high, (a - high.astype(f32)).astype(bf16)


def three_products(a, table_ref):
    high, low = split(a)
    first = table_ref[0]
    return dot(high, first) + dot(low, first) + dot(high, table_ref[1])


def spread(lines, twist_ref, fold_ref):
    half = lines.shape[1] // 2
    real, imag = lines[:LINES], lines[LINES:]
    cos, sin = twist_ref[0], twist_ref[1]
    turned_real = real * cos + imag * sin
    turned_imag = imag * cos - real * sin
    even_real = turned_real[:, :half] + turned_real[:, half:]
    even_imag = turned_imag[:, :half] + turned_imag[:, half:]
    diff_real = turned_real[:, :half] - turned_real[:, half:]
    diff_imag = turned_imag[:, :half] - turned_imag[:, half:]
    fold_cos, fold_sin = fold_ref[0:1], fold_ref[1:2]
    odd_real = diff_real * fold_cos + diff_imag * fold_sin
    odd_imag = diff_imag * fold_cos - diff_real * fold_sin
    return jnp.concatenate(
        [
            jnp.concatenate([even_real, even_imag], axis=1),
            jnp.concatenate([odd_real, odd_imag], axis=1),
        ],
        axis=0,
    )


def gather_back(rows, twist_ref, fold_ref):
    half = rows.shape[1] // 2
    even_real, even_imag = rows[:LINES, :half], rows[:LINES, half:]
    odd_real, odd_imag = rows[LINES:, :half], rows[LINES:, half:]
    fold_cos, fold_sin = fold_ref[0:1], fold_ref[1:2]
    rest_real = odd_real * fold_cos - odd_imag * fold_sin
    rest_imag = odd_imag * fold_cos + odd_real * fold_sin
    real = jnp.concatenate([even_real + rest_real, even_real - rest_real], axis=1)
    imag = jnp.concatenate([even_imag + rest_imag, even_imag - rest_imag], axis=1)
    cos, sin = twist_ref[0], twist_ref[1]
    return jnp.concatenate([real * cos - imag * sin, imag * cos + real * sin], axis=0)


def fill(flat, planes):
    blocks, channels, width = planes.shape
    rows = planes.reshape(blocks * channels, width)
    for q in range(width // 128):
        flat[q] = rows[:, 128 * q : 128 * (q + 1)]


def channel_of(flat, channel, blocks, channels):
    place = pl.ds(channel, blocks, stride=channels)
    return jnp.concatenate([flat[q, place, :] for q in range(flat.shape[0])], axis=1)


def taps_kernel(taps_ref, lead_ref, twist_ref, fold_ref, forward_ref, spec_ref, flat):
    blocks, channels, width = taps_ref.shape
    fill(flat, taps_ref[...].astype(f32))

    def body(pair, carry):
        rows = []
        for k in range(2):
            plane = channel_of(flat, 2 * pair + k, blocks, channels).astype(bf16)
            lines = dot(lead_ref[...], jnp.concatenate([plane, plane], axis=0))
            rows.append(spread(lines, twist_ref, fold_ref))
        spec_ref[pair] = three_products(jnp.concatenate(rows, axis=0), forward_ref)
        return carry

    lax.fori_loop(0, channels // 2, body, 0)


def conv_kernel(
    gain_ref, parts_ref, spec_ref, lead_ref, tail_ref, twist_ref, fold_ref, forward_ref, backward_ref,
    out_ref, flat, mixed,
):
    _, blocks, channels, width = parts_ref.shape
    half = width // 2
    fill(flat, parts_ref[0].astype(f32) + parts_ref[1].astype(f32))
    spare = tail_ref.shape[1] - 6 * LINES

    def body(pair, carry):
        rows = []
        for k in range(2):
            high, low = split(channel_of(flat, 2 * pair + k, blocks, channels))
            lines = dot(lead_ref[...], jnp.concatenate([high, low, high], axis=0))
            rows.append(spread(lines, twist_ref, fold_ref))
        signal = three_products(jnp.concatenate(rows, axis=0), forward_ref)
        taps = spec_ref[pair]
        real, imag = signal[:, :half], signal[:, half:]
        taps_real, taps_imag = taps[:, :half], taps[:, half:]
        product = jnp.concatenate(
            [real * taps_real - imag * taps_imag, real * taps_imag + imag * taps_real], axis=1
        )
        back = three_products(product, backward_ref)
        for k in range(2):
            lines = gather_back(back[2 * LINES * k : 2 * LINES * (k + 1)], twist_ref, fold_ref)
            high, low = split(lines)
            pad = jnp.zeros((spare, width), bf16)
            value = dot(tail_ref[...], jnp.concatenate([high, low, high, pad], axis=0))
            place = pl.ds(2 * pair + k, blocks, stride=channels)
            gain = gain_ref[2 * pair + k]
            for q in range(width // 128):
                part = value[:, 128 * q : 128 * (q + 1)]
                mixed[q, place, :] = part + gain * flat[q, place, :]
        return carry

    lax.fori_loop(0, channels // 2, body, 0)
    for q in range(width // 128):
        result = mixed[q].astype(bf16).reshape(blocks, channels, 128)
        for copy in range(out_ref.shape[0]):
            out_ref[copy, :, :, 128 * q : 128 * (q + 1)] = result


def project_kernel(tokens_ref, weight_ref, out_ref):
    out_ref[...] = dot(tokens_ref[...], weight_ref[...]).T.astype(bf16)


def out_kernel(place_ref, mixed_ref, own_ref, near_ref, far_ref, out_ref, turned):
    group, core = place_ref[0], place_ref[1]
    rows = own_ref.shape[0]
    part = near_ref.shape[0]

    @pl.when(pl.program_id(0) == 0)
    def _():
        other = (1 - group) * rows
        starts = [group * rows, other + core * part, other + (1 - core) * part]
        at = 0
        for start, size in zip(starts, [rows, part, part]):
            piece = mixed_ref[pl.ds(pl.multiple_of(start, part), size), :]
            turned[:, at : at + size] = piece.T
            at += size

    value = dot(turned[:, :rows], own_ref[...])
    value += dot(turned[:, rows : rows + part], near_ref[...])
    value += dot(turned[:, rows + part :], far_ref[...])
    out_ref[...] = value.astype(bf16)


def vmem(limit):
    return pltpu.CompilerParams(vmem_limit_bytes=limit * MIB)


def whole():
    return pl.BlockSpec(memory_space=pltpu.VMEM)


def permutes(x_size, z_size):
    def place(y, x, z, core):
        return (((y % 2 * x_size + x) * z_size + z) * 2 + core) * 2 + y // 2

    across, cores = [], []
    for y in range(4):
        for x in range(x_size):
            for z in range(z_size):
                for core in range(2):
                    across.append((place(y, x, z, core), place(3 - y, x, z, core)))
                    cores.append((place(y, x, z, core), place(y, x, z, 1 - core)))
    return across, cores


def shards(tokens, in_weight, filter_taps, skip_gain, out_weight):
    ctx, ch = lax.axis_size("ctx"), lax.axis_size("ch")
    devices = ctx * ch
    position, features = tokens.shape
    width = in_weight.shape[1]
    channels = width // devices
    here, group = lax.axis_index("ctx"), lax.axis_index("ch")
    core = here % 2
    table = {k: jnp.asarray(v) for k, v in tables(ctx, position).items()}

    rows = out_weight.shape[0]
    across, cores = permutes(4, 4)
    wanted = lax.dynamic_slice(
        out_weight, (core * (rows // 2), (1 - group) * features), (rows // 2, features)
    )
    near = lax.ppermute(wanted, ("ctx", "ch"), across)
    far = lax.ppermute(near, ("ctx", "ch"), cores)

    taps = filter_taps.T.astype(bf16).reshape(ctx, channels, position)
    taps = lax.all_to_all(taps, "ctx", split_axis=0, concat_axis=0, tiled=True)

    block = 256
    partial_value = pl.pallas_call(
        project_kernel,
        grid=(width // block,),
        in_specs=[
            pl.BlockSpec((position, features), lambda i: (0, 0)),
            pl.BlockSpec((features, block), lambda i: (0, i)),
        ],
        out_specs=pl.BlockSpec((block, position), lambda i: (i, 0)),
        out_shape=jax.ShapeDtypeStruct((width, position), bf16),
        compiler_params=vmem(40),
        cost_estimate=pl.CostEstimate(
            flops=2 * position * features * width, bytes_accessed=13 * MIB, transcendentals=0
        ),
    )(tokens, in_weight)

    line_rows = 4 * LINES
    lanes = (position // 128, ctx * channels, 128)
    spec = pl.pallas_call(
        taps_kernel,
        in_specs=[whole()] * 5,
        out_specs=whole(),
        out_shape=jax.ShapeDtypeStruct((channels // 2, line_rows, position), f32),
        scratch_shapes=[pltpu.VMEM(lanes, f32)],
        compiler_params=vmem(40),
        cost_estimate=pl.CostEstimate(flops=4 * 10**9, bytes_accessed=4 * MIB, transcendentals=0),
    )(taps, table["lead_taps"], table["twist"], table["fold"], table["forward"])

    parts = lax.all_to_all(
        partial_value.reshape(devices, channels, position),
        ("ch", "ctx"), split_axis=0, concat_axis=0, tiled=True,
    ).reshape(ch, ctx, channels, position)

    gain = lax.dynamic_slice(skip_gain, (here * channels,), (channels,))
    mixed = pl.pallas_call(
        conv_kernel,
        in_specs=[pl.BlockSpec(memory_space=pltpu.SMEM)] + [whole()] * 8,
        out_specs=whole(),
        out_shape=jax.ShapeDtypeStruct((ch, ctx, channels, position), bf16),
        scratch_shapes=[pltpu.VMEM(lanes, f32)] * 2,
        compiler_params=vmem(40),
        cost_estimate=pl.CostEstimate(flops=8 * 10**9, bytes_accessed=8 * MIB, transcendentals=0),
    )(
        gain, parts, spec, table["lead_signal"], table["tail"], table["twist"], table["fold"],
        table["forward"], table["backward"],
    )

    mixed = lax.all_to_all(
        mixed.reshape(devices, channels, position),
        ("ch", "ctx"), split_axis=0, concat_axis=0, tiled=True,
    ).reshape(width, position)

    step = 512
    steps = features // step
    return pl.pallas_call(
        out_kernel,
        grid_spec=pltpu.PrefetchScalarGridSpec(
            num_scalar_prefetch=1,
            grid=(steps,),
            in_specs=[
                pl.BlockSpec((width, position), lambda i, place: (0, 0)),
                pl.BlockSpec((rows, step), lambda i, place: (0, place[0] * steps + i)),
                pl.BlockSpec((rows // 2, step), lambda i, place: (0, i)),
                pl.BlockSpec((rows // 2, step), lambda i, place: (0, i)),
            ],
            out_specs=pl.BlockSpec((position, step), lambda i, place: (0, i)),
            scratch_shapes=[pltpu.VMEM((position, width), bf16)],
        ),
        out_shape=jax.ShapeDtypeStruct((position, features), bf16),
        compiler_params=vmem(40),
        cost_estimate=pl.CostEstimate(
            flops=2 * position * features * width, bytes_accessed=13 * MIB, transcendentals=0
        ),
    )(jnp.stack([group, core]).astype(jnp.int32), mixed, out_weight, near, far)


def solution(mesh):
    return jax.shard_map(
        shards,
        mesh=mesh,
        in_specs=(P("ctx", "ch"), P("ch", None), P("ctx", "ch"), P("ch"), P("ch", None)),
        out_specs=P("ctx", "ch"),
        check_vma=False,
    )
```

```python
import numpy as np
import ml_dtypes
import jax
import jax.numpy as jnp
from jax import lax
from jax.experimental import pallas as pl
from jax.experimental.pallas import tpu as pltpu
from jax.sharding import PartitionSpec as P

bf16 = jnp.bfloat16
f32 = jnp.float32
MIB = 1024 * 1024
LINES = 72
GROUP = 4
CHUNK = 512
PIECES = 4


def split_table(table):
    high = table.astype(ml_dtypes.bfloat16)
    low = (table - high.astype(np.float64)).astype(ml_dtypes.bfloat16)
    return high, low


def tables(blocks, width):
    period = 2 * blocks * width
    quarter = width // 4
    freq = np.arange(LINES)[:, None]
    live = (freq <= blocks).astype(np.float64)
    angle = 2.0 * np.pi * (freq * np.arange(blocks)[None, :] % (2 * blocks)) / (2 * blocks)
    lead = np.concatenate([np.cos(angle) * live, -np.sin(angle) * live], axis=0)
    lead_high, lead_low = split_table(lead)
    weight = np.where((freq == 0) | (freq == blocks), 1.0, 2.0) * live / period
    tail = np.concatenate([np.cos(angle) * weight, np.sin(angle) * weight], axis=0).T
    tail_high, tail_low = split_table(tail)
    spare = np.zeros((blocks, -6 * LINES % 256), ml_dtypes.bfloat16)
    turn = 2.0 * np.pi * freq * np.arange(width)[None, :] / period
    fold = 2.0 * np.pi * np.arange(4)[:, None] * np.arange(quarter)[None, :] / width
    index = np.arange(quarter)
    line = 2.0 * np.pi * (index[:, None] * index[None, :] % quarter) / quarter
    cos, sin = np.cos(line), np.sin(line)
    line_high, line_low = split_table(np.block([[cos, -sin], [sin, cos]]))
    return dict(
        lead_signal=np.concatenate([lead_high, lead_high, lead_low], axis=1),
        lead_taps=np.concatenate([lead_high, lead_low], axis=1),
        tail=np.concatenate([tail_high, tail_high, tail_low, spare], axis=1),
        twist=np.stack([np.cos(turn), np.sin(turn)]).astype(np.float32),
        fold=np.concatenate([np.cos(fold), np.sin(fold)]).astype(np.float32),
        line=np.concatenate([line_high, line_high, line_low], axis=0),
    )


def dot(a, b):
    return jnp.dot(a, b, preferred_element_type=f32)


def split(a):
    high = a.astype(bf16)
    return high, (a - high.astype(f32)).astype(bf16)


def line_transform(rows, line_ref):
    high, low = split(rows)
    return dot(jnp.concatenate([high, low, high], axis=1), line_ref[...])


def turn_back(real, imag, cos, sin):
    return real * cos + imag * sin, imag * cos - real * sin


def butterfly(parts):
    (ar, ai), (br, bi), (cr, ci), (dr, di) = parts
    sr, si, er, ei = ar + cr, ai + ci, ar - cr, ai - ci
    tr, ti, fr, fi = br + dr, bi + di, br - dr, bi - di
    return [(sr + tr, si + ti), (er + fi, ei - fr), (sr - tr, si - ti), (er - fi, ei + fr)]


def spread(lines, twist_ref, fold_ref):
    quarter = lines.shape[1] // 4
    parts = []
    for p in range(4):
        at = slice(quarter * p, quarter * (p + 1))
        parts.append(
            turn_back(lines[:LINES, at], lines[LINES:, at], twist_ref[0, :, at], twist_ref[1, :, at])
        )
    rows = []
    for r, (real, imag) in enumerate(butterfly(parts)):
        if r:
            real, imag = turn_back(real, imag, fold_ref[r : r + 1], fold_ref[r + 4 : r + 5])
        rows.append(jnp.concatenate([real, imag], axis=1))
    return rows


def gather_back(rows, twist_ref, fold_ref):
    quarter = rows.shape[1] // 2
    got = []
    for r in range(4):
        at = slice(LINES * r, LINES * (r + 1))
        real, imag = rows[at, :quarter], rows[at, quarter:]
        if r:
            real, imag = turn_back(real, imag, fold_ref[r : r + 1], fold_ref[r + 4 : r + 5])
        got.append((real, imag))
    reals, imags = [], []
    for p, (real, imag) in enumerate(butterfly(got)):
        at = slice(quarter * p, quarter * (p + 1))
        real, imag = turn_back(real, imag, twist_ref[0, :, at], twist_ref[1, :, at])
        reals.append(real)
        imags.append(imag)
    return jnp.concatenate(
        [jnp.concatenate(reals, axis=1), jnp.concatenate(imags, axis=1)], axis=0
    )


def fill(flat, planes):
    blocks, channels, width = planes.shape
    rows = planes.reshape(blocks * channels, width)
    for q in range(width // 128):
        flat[q] = rows[:, 128 * q : 128 * (q + 1)]


def channel_of(flat, channel, blocks, channels):
    place = pl.ds(channel, blocks, stride=channels)
    return jnp.concatenate([flat[q, place, :] for q in range(flat.shape[0])], axis=1)


def where():
    here = lax.axis_index("ctx")
    return lax.axis_index("ch"), here & 1, (here >> 3 & 1) * 2 + (here >> 1 & 1)


def start_all(pairs, sems):
    copies = [pltpu.make_async_copy(a, b, sems.at[i]) for i, (a, b) in enumerate(pairs)]
    for copy in copies:
        copy.start()
    return copies


def spectrum_kernel(
    taps_ref, lead_hbm, twist_hbm, fold_hbm, line_hbm, spec_hbm,
    lead_ref, twist_ref, fold_ref, line_ref, flat, spec_ref, sems, out_sems,
):
    blocks, channels, width = taps_ref.shape
    copies = start_all(
        [(lead_hbm, lead_ref), (twist_hbm, twist_ref), (fold_hbm, fold_ref), (line_hbm, line_ref)],
        sems,
    )
    fill(flat, taps_ref[...].astype(f32))
    for copy in copies:
        copy.wait()
    stores = []
    for step in range(channels // GROUP):
        rows = []
        for c in range(GROUP * step, GROUP * (step + 1)):
            plane = channel_of(flat, c, blocks, channels).astype(bf16)
            lines = dot(lead_ref[...], jnp.concatenate([plane, plane], axis=0))
            rows += spread(lines, twist_ref, fold_ref)
        spec_ref[step] = line_transform(jnp.concatenate(rows, axis=0), line_ref)
        store = pltpu.make_async_copy(spec_ref.at[step], spec_hbm.at[step], out_sems.at[step])
        store.start()
        stores.append(store)
    for store in stores:
        store.wait()


def conv_kernel(
    gain_ref, parts_ref, spec_hbm, lead_hbm, tail_hbm, twist_hbm, fold_hbm, line_hbm,
    out_hbm,
    spec_ref, lead_ref, tail_ref, twist_ref, fold_ref, line_ref,
    flat, mixed, out_ref, sems, out_sems,
):
    _, blocks, channels, width = parts_ref.shape
    quarter = width // 4
    first_gain = lax.axis_index("ctx") * channels
    copies = start_all(
        [
            (lead_hbm, lead_ref), (twist_hbm, twist_ref), (fold_hbm, fold_ref),
            (line_hbm, line_ref), (spec_hbm, spec_ref), (tail_hbm, tail_ref),
        ],
        sems,
    )
    fill(flat, parts_ref[0].astype(f32) + parts_ref[1].astype(f32))
    for copy in copies[:4]:
        copy.wait()
    spare = tail_ref.shape[1] - 6 * LINES
    size = 4 * LINES

    for step in range(channels // GROUP):
        held = range(GROUP * step, GROUP * (step + 1))
        rows = []
        for c in held:
            high, low = split(channel_of(flat, c, blocks, channels))
            lines = dot(lead_ref[...], jnp.concatenate([high, low, high], axis=0))
            rows += spread(lines, twist_ref, fold_ref)
        spec = line_transform(jnp.concatenate(rows, axis=0), line_ref)
        if step == 0:
            for copy in copies[4:]:
                copy.wait()
        products = []
        for k, c in enumerate(held):
            at = slice(size * k, size * (k + 1))
            real, imag = spec[at, :quarter], spec[at, quarter:]
            taps_real = spec_ref[step, at, :quarter] + gain_ref[first_gain + c]
            taps_imag = spec_ref[step, at, quarter:]
            products.append(
                jnp.concatenate(
                    [real * taps_real - imag * taps_imag, -(real * taps_imag + imag * taps_real)],
                    axis=1,
                )
            )
        back = line_transform(jnp.concatenate(products, axis=0), line_ref)
        for k, c in enumerate(held):
            lines = gather_back(back[size * k : size * (k + 1)], twist_ref, fold_ref)
            high, low = split(lines)
            pad = jnp.zeros((spare, width), bf16)
            value = dot(tail_ref[...], jnp.concatenate([high, low, high, pad], axis=0))
            place = pl.ds(c, blocks, stride=channels)
            for q in range(width // 128):
                mixed[q, place, :] = value[:, 128 * q : 128 * (q + 1)]

    for q in range(width // 128):
        result = mixed[q].astype(bf16).reshape(blocks, channels, 128)
        out_ref[:, :, 128 * q : 128 * (q + 1)] = result
    for copy in start_all([(out_ref, out_hbm.at[k]) for k in range(out_hbm.shape[0])], out_sems):
        copy.wait()


def prepare_kernel(
    taps_hbm, weight_hbm, taps_out_hbm, first_hbm, last_hbm, taps_ref, taps_out_ref, pieces_ref, sems
):
    group, core, first = where()
    taps_load = pltpu.make_async_copy(taps_hbm, taps_ref, sems.at[0])
    taps_load.start()
    size, columns = first_hbm.shape
    at = pl.ds(pl.multiple_of((1 - group) * columns, columns), columns)
    loads, stores = [], []
    for i, (piece, which) in enumerate([(first_hbm, first), (last_hbm, first ^ 3)]):
        rows = pl.ds(pl.multiple_of((core * PIECES + which) * size, size), size)
        loads.append(pltpu.make_async_copy(weight_hbm.at[rows, at], pieces_ref.at[i], sems.at[2 + i]))
        stores.append(pltpu.make_async_copy(pieces_ref.at[i], piece, sems.at[4 + i]))
        loads[i].start()
    taps_load.wait()
    taps_out_ref[...] = taps_ref[...].astype(bf16).T
    stores.append(pltpu.make_async_copy(taps_out_ref, taps_out_hbm, sems.at[1]))
    stores[2].start()
    for i in range(2):
        loads[i].wait()
        stores[i].start()
    for store in stores:
        store.wait()


def fence_kernel(value_ref, after_ref, out_ref):
    pass


def project_kernel(
    tokens_hbm, weight_hbm, out_hbm, tokens_ref, weight_ref, total, out_ref,
    token_sems, weight_sems, out_sems,
):
    features = tokens_ref.shape[1]
    width = weight_ref.shape[1]
    steps = features // CHUNK
    parts = 4
    loads = []
    for i in range(steps):
        at = pl.ds(i * CHUNK, CHUNK)
        pair = (
            pltpu.make_async_copy(tokens_hbm.at[:, at], tokens_ref.at[:, at], token_sems.at[i]),
            pltpu.make_async_copy(weight_hbm.at[at], weight_ref.at[at], weight_sems.at[i]),
        )
        for copy in pair:
            copy.start()
        loads.append(pair)
    stores = []
    for i in range(steps):
        for copy in loads[i]:
            copy.wait()
        at = slice(i * CHUNK, (i + 1) * CHUNK)
        for c in range(parts):
            cols = slice(c * width // parts, (c + 1) * width // parts)
            term = dot(tokens_ref[:, at], weight_ref[at, cols])
            if i == 0:
                total[:, cols] = term
            elif i < steps - 1:
                total[:, cols] += term
            else:
                out_ref[cols, :] = (total[:, cols] + term).astype(bf16).T
                rows = pl.ds(c * width // parts, width // parts)
                store = pltpu.make_async_copy(out_ref.at[rows], out_hbm.at[rows], out_sems.at[c])
                store.start()
                stores.append(store)
    for store in stores:
        store.wait()


def weights_kernel(own_hbm, *rest):
    pieces, (out_hbm, held_ref, sems, out_sems) = rest[:-4], rest[-4:]
    rows = own_hbm.shape[0]
    blocks, _, columns = out_hbm.shape
    size = rows // len(pieces)
    group = where()[0]
    at = pl.ds(pl.multiple_of(group * (blocks * columns), columns), blocks * columns)
    pairs = [(own_hbm.at[:, at], held_ref.at[pl.ds(0, rows)])]
    for i, piece in enumerate(pieces):
        pairs.append((piece, held_ref.at[pl.ds(rows + i * size, size)]))
    for copy in start_all(pairs, sems):
        copy.wait()
    stores = start_all(
        [(held_ref.at[:, pl.ds(b * columns, columns)], out_hbm.at[b]) for b in range(blocks)],
        out_sems,
    )
    for copy in stores:
        copy.wait()


def out_kernel(mixed_ref, weight_hbm, out_hbm, turned, weight_ref, out_ref, sems, out_sems):
    steps, _, columns = weight_ref.shape
    loads = start_all([(weight_hbm.at[i], weight_ref.at[i]) for i in range(steps)], sems)
    group, core, first = where()
    width, position = mixed_ref.shape
    rows = width // 2
    size = rows // (2 * PIECES)
    own = mixed_ref[pl.ds(pl.multiple_of(group * rows, rows), rows), :]
    turned[:, :rows] = own.T
    pieces = []
    for half in (core, 1 - core):
        for flip in range(PIECES):
            start = (1 - group) * rows + half * (rows // 2) + (first ^ flip) * size
            pieces.append(mixed_ref[pl.ds(pl.multiple_of(start, size), size), :])
    turned[:, rows:] = jnp.concatenate(pieces, axis=0).T
    stores = []
    for i in range(steps):
        loads[i].wait()
        at = slice(i * columns, (i + 1) * columns)
        out_ref[:, at] = dot(turned[...], weight_ref[i]).astype(bf16)
        span = pl.ds(i * columns, columns)
        store = pltpu.make_async_copy(out_ref.at[:, span], out_hbm.at[:, span], out_sems.at[i])
        store.start()
        stores.append(store)
    for store in stores:
        store.wait()


def vmem(limit):
    return pltpu.CompilerParams(vmem_limit_bytes=limit * MIB)


def cost(flops, size):
    return pl.CostEstimate(flops=flops, bytes_accessed=size, transcendentals=0)


ANY = pl.BlockSpec(memory_space=pl.ANY)
SMEM = pl.BlockSpec(memory_space=pltpu.SMEM)
VMEM = pl.BlockSpec(memory_space=pltpu.VMEM)


def partners(move):
    def place(y, x, z, core):
        return (((y % 2 * 4 + x) * 4 + z) * 2 + core) * 2 + y // 2

    spots = [(y, x, z, c) for y in range(4) for x in range(4) for z in range(4) for c in range(2)]
    return [(place(*spot), place(*move(*spot))) for spot in spots]


def shards(tokens, in_weight, filter_taps, skip_gain, out_weight):
    ctx, ch = lax.axis_size("ctx"), lax.axis_size("ch")
    devices = ctx * ch
    position, features = tokens.shape
    width = in_weight.shape[1]
    channels = width // devices
    rows = out_weight.shape[0]
    table = {k: jnp.asarray(v) for k, v in tables(ctx, position).items()}

    across = partners(lambda y, x, z, c: (3 - y, x, z, c))
    along_x = partners(lambda y, x, z, c: (y, x ^ 1, z, c))
    along_z = partners(lambda y, x, z, c: (y, x, z ^ 1, c))
    other_core = partners(lambda y, x, z, c: (y, x, z, 1 - c))
    both = ("ctx", "ch")
    size = rows // (2 * PIECES)
    piece = jax.ShapeDtypeStruct((size, features), bf16)

    taps, first_piece, last_piece = pl.pallas_call(
        prepare_kernel,
        in_specs=[ANY, ANY],
        out_specs=[ANY] * 3,
        out_shape=[jax.ShapeDtypeStruct((width // ch, position), bf16), piece, piece],
        scratch_shapes=[
            pltpu.VMEM((position, width // ch), f32),
            pltpu.VMEM((width // ch, position), bf16),
            pltpu.VMEM((2, size, features), bf16),
            pltpu.SemaphoreType.DMA((6,)),
        ],
        compiler_params=vmem(60),
        cost_estimate=cost(0, 4 * MIB),
    )(filter_taps, out_weight)

    mine = lax.ppermute(first_piece, both, across)
    taps = lax.all_to_all(
        taps.reshape(ctx, channels, position), "ctx", split_axis=0, concat_axis=0, tiled=True
    )

    partial_value = pl.pallas_call(
        project_kernel,
        in_specs=[ANY] * 2,
        out_specs=ANY,
        out_shape=jax.ShapeDtypeStruct((width, position), bf16),
        scratch_shapes=[
            pltpu.VMEM((position, features), bf16),
            pltpu.VMEM((features, width), bf16),
            pltpu.VMEM((position, width), f32),
            pltpu.VMEM((width, position), bf16),
            pltpu.SemaphoreType.DMA((features // CHUNK,)),
            pltpu.SemaphoreType.DMA((features // CHUNK,)),
            pltpu.SemaphoreType.DMA((4,)),
        ],
        compiler_params=vmem(60),
        cost_estimate=cost(2 * position * features * width, 14 * MIB),
    )(tokens, in_weight)

    partial_value = pl.pallas_call(
        fence_kernel,
        in_specs=[ANY] * 2,
        out_specs=ANY,
        out_shape=jax.ShapeDtypeStruct((width, position), bf16),
        input_output_aliases={0: 0},
        compiler_params=vmem(60),
    )(partial_value, mine)

    parts = lax.all_to_all(
        partial_value.reshape(devices, channels, position),
        ("ch", "ctx"), split_axis=0, concat_axis=0, tiled=True,
    ).reshape(ch, ctx, channels, position)

    by_x = lax.ppermute(mine, both, along_x)
    by_z = lax.ppermute(mine, both, along_z)
    last = lax.ppermute(last_piece, both, across)
    pieces = [mine, by_z, by_x, last]
    pieces = pieces + [lax.ppermute(p, both, other_core) for p in pieces]

    lanes = (position // 128, ctx * channels, 128)
    spec_shape = (channels // GROUP, GROUP * 4 * LINES, position // 2)
    used = [table[k] for k in ("lead_taps", "twist", "fold", "line")]
    spec = pl.pallas_call(
        spectrum_kernel,
        in_specs=[VMEM] + [ANY] * 4,
        out_specs=ANY,
        out_shape=jax.ShapeDtypeStruct(spec_shape, f32),
        scratch_shapes=[
            *[pltpu.VMEM(t.shape, t.dtype) for t in used],
            pltpu.VMEM(lanes, f32),
            pltpu.VMEM(spec_shape, f32),
            pltpu.SemaphoreType.DMA((4,)),
            pltpu.SemaphoreType.DMA((channels // GROUP,)),
        ],
        compiler_params=vmem(58),
        cost_estimate=cost(4 * 10**9, 4 * MIB),
    )(taps, *used)

    used = [table[k] for k in ("lead_signal", "tail", "twist", "fold", "line")]
    mixed = pl.pallas_call(
        conv_kernel,
        in_specs=[SMEM, VMEM] + [ANY] * 6,
        out_specs=ANY,
        out_shape=jax.ShapeDtypeStruct((ch, ctx, channels, position), bf16),
        scratch_shapes=[
            pltpu.VMEM(spec_shape, f32),
            *[pltpu.VMEM(t.shape, t.dtype) for t in used],
            pltpu.VMEM(lanes, f32),
            pltpu.VMEM(lanes, f32),
            pltpu.VMEM((ctx, channels, position), bf16),
            pltpu.SemaphoreType.DMA((6,)),
            pltpu.SemaphoreType.DMA((ch,)),
        ],
        compiler_params=vmem(58),
        cost_estimate=cost(8 * 10**9, 6 * MIB),
    )(skip_gain, parts, spec, *used)

    mixed = lax.all_to_all(
        mixed.reshape(devices, channels, position),
        ("ch", "ctx"), split_axis=0, concat_axis=0, tiled=True,
    ).reshape(width, position)

    steps = features // 512
    weights = pl.pallas_call(
        weights_kernel,
        in_specs=[ANY] * (1 + 2 * PIECES),
        out_specs=ANY,
        out_shape=jax.ShapeDtypeStruct((steps, width, features // steps), bf16),
        scratch_shapes=[
            pltpu.VMEM((width, features), bf16),
            pltpu.SemaphoreType.DMA((1 + 2 * PIECES,)),
            pltpu.SemaphoreType.DMA((steps,)),
        ],
        compiler_params=vmem(60),
        cost_estimate=cost(0, 16 * MIB),
    )(out_weight, *pieces)

    return pl.pallas_call(
        out_kernel,
        in_specs=[VMEM, ANY],
        out_specs=ANY,
        out_shape=jax.ShapeDtypeStruct((position, features), bf16),
        scratch_shapes=[
            pltpu.VMEM((position, width), bf16),
            pltpu.VMEM((steps, width, features // steps), bf16),
            pltpu.VMEM((position, features), bf16),
            pltpu.SemaphoreType.DMA((steps,)),
            pltpu.SemaphoreType.DMA((steps,)),
        ],
        compiler_params=vmem(58),
        cost_estimate=cost(2 * position * features * width, 13 * MIB),
    )(mixed, weights)


def solution(mesh):
    return jax.shard_map(
        shards,
        mesh=mesh,
        in_specs=(P("ctx", "ch"), P("ch", None), P("ctx", "ch"), P("ch"), P("ch", None)),
        out_specs=P("ctx", "ch"),
        check_vma=False,
    )
```

```python
import numpy as np
import ml_dtypes
import jax
import jax.numpy as jnp
from jax import lax
from jax.experimental import pallas as pl
from jax.experimental.pallas import tpu as pltpu
from jax.sharding import PartitionSpec as P

bf16 = jnp.bfloat16
f32 = jnp.float32
MIB = 1024 * 1024
TILE = 16
GROUP = 4
CHUNK = 512
SPARE = 12
LAST_PARTS = 4
PIECES = 4


def split_table(table):
    high = table.astype(ml_dtypes.bfloat16)
    low = (table - high.astype(np.float64)).astype(ml_dtypes.bfloat16)
    return high, low


def tables(blocks, width):
    period = 2 * blocks * width
    quarter = width // 4
    freq = np.arange(blocks)[:, None]
    angle = 2.0 * np.pi * (freq * np.arange(blocks)[None, :] % (2 * blocks)) / (2 * blocks)
    lead_high, lead_low = split_table(np.concatenate([np.cos(angle), -np.sin(angle)], axis=0))
    weight = np.where(freq == 0, 1.0, 2.0) / period
    cosines, sines = np.cos(angle) * weight, np.sin(angle) * weight
    sines[0] = (1.0 - 2.0 * (np.arange(blocks) % 2)) / period
    tail_high, tail_low = split_table(np.concatenate([cosines, sines], axis=0).T)
    turned = np.concatenate([freq, np.full((TILE, 1), blocks)])
    turn = 2.0 * np.pi * turned * np.arange(width)[None, :] / period
    fold = 2.0 * np.pi * np.arange(4)[:, None] * np.arange(quarter)[None, :] / width
    index = np.arange(quarter)
    line = 2.0 * np.pi * (index[:, None] * index[None, :] % quarter) / quarter
    cos, sin = np.cos(line), np.sin(line)
    line_high, line_low = split_table(np.block([[cos, -sin], [sin, cos]]))
    parts = [
        line_high,
        line_low,
        np.concatenate([lead_high, lead_high, lead_low], axis=1),
        np.concatenate([lead_high, lead_low], axis=1),
        np.block([[tail_high, tail_high], [tail_low, np.zeros_like(tail_low)]]),
        *np.split(np.cos(turn), 2, axis=1),
        *np.split(np.sin(turn), 2, axis=1),
        np.concatenate([np.cos(fold), np.sin(fold)]),
    ]
    columns = line_high.shape[1]
    return np.concatenate(
        [np.pad(p.astype(np.float32), ((0, 0), (0, columns - p.shape[1]))) for p in parts]
    )


def unpack(table_ref, blocks, line_ref, twist_ref):
    columns = line_ref.shape[1]
    line_ref[:columns] = table_ref[:columns].astype(bf16)
    line_ref[columns:] = table_ref[: 2 * columns].astype(bf16)
    at = 2 * columns
    leads = []
    for use in (3 * blocks, 2 * blocks, 4 * blocks):
        leads.append(table_ref[at : at + 2 * blocks, :use].astype(bf16))
        at += 2 * blocks
    rows = twist_ref.shape[1]
    for i in range(2):
        for k in range(2):
            twist_ref[i, :, columns * k : columns * (k + 1)] = table_ref[at : at + rows]
            at += rows
    return (*leads, table_ref[at : at + 8, : columns // 2])


def dot(a, b):
    return jnp.dot(a, b, preferred_element_type=f32)


def split(a):
    high = a.astype(bf16)
    return high, (a - high.astype(f32)).astype(bf16)


def turn_back(real, imag, cos, sin):
    return real * cos + imag * sin, imag * cos - real * sin


def butterfly(parts):
    (ar, ai), (br, bi), (cr, ci), (dr, di) = parts
    sr, si, er, ei = ar + cr, ai + ci, ar - cr, ai - ci
    tr, ti, fr, fi = br + dr, bi + di, br - dr, bi - di
    return [(sr + tr, si + ti), (er + fi, ei - fr), (sr - tr, si - ti), (er - fi, ei + fr)]


def put_rows(rows_ref, at, value):
    high, low = split(value)
    size = value.shape[1]
    span = pl.ds(at, value.shape[0])
    rows_ref[span, :size] = high
    rows_ref[span, size : 2 * size] = low


def transform_rows(rows_ref, at, count, line_ref):
    size = line_ref.shape[1]
    span = pl.ds(at, count)
    both = dot(rows_ref[span, :], line_ref[: 2 * size, :])
    return both + dot(rows_ref[span, :size], line_ref[2 * size :, :])


def spread(real, imag, freqs, rows_ref, at, twist_ref, fold):
    quarter = real.shape[1] // 4
    parts = []
    for p in range(4):
        lanes = slice(quarter * p, quarter * (p + 1))
        cos, sin = twist_ref[0, freqs, lanes], twist_ref[1, freqs, lanes]
        if imag is None:
            parts.append((real[:, lanes] * cos, -real[:, lanes] * sin))
        else:
            parts.append(turn_back(real[:, lanes], imag[:, lanes], cos, sin))
    for r, (a, b) in enumerate(butterfly(parts)):
        if r:
            a, b = turn_back(a, b, fold[r : r + 1], fold[r + 4 : r + 5])
        put_rows(rows_ref, at + TILE * r, jnp.concatenate([a, b], axis=1))


def gather_back(back_ref, at, freqs, twist_ref, fold):
    quarter = back_ref.shape[1] // 2
    got = []
    for r in range(4):
        span = pl.ds(at + TILE * r, TILE)
        a, b = back_ref[span, :quarter], back_ref[span, quarter:]
        if r:
            a, b = turn_back(a, b, fold[r : r + 1], fold[r + 4 : r + 5])
        got.append((a, b))
    reals, imags = [], []
    for p, (a, b) in enumerate(butterfly(got)):
        lanes = slice(quarter * p, quarter * (p + 1))
        a, b = turn_back(a, b, twist_ref[0, freqs, lanes], twist_ref[1, freqs, lanes])
        reals.append(a)
        imags.append(b)
    return jnp.concatenate(reals, axis=1), jnp.concatenate(imags, axis=1)


def where():
    here = lax.axis_index("ctx")
    return lax.axis_index("ch"), here & 1, here >> 3 & 3, here >> 1 & 3


def held_pieces(x, z):
    first = (x & 1) * 2 + (z & 1)
    return [first ^ flip for flip in range(PIECES)]


def start_all(pairs, sems):
    copies = [pltpu.make_async_copy(a, b, sems.at[i]) for i, (a, b) in enumerate(pairs)]
    for copy in copies:
        copy.start()
    return copies


def forward(load, last, lead, lines_ref, rows_ref, spec_ref, twist_ref, fold, line_ref):
    channels = lines_ref.shape[0]
    blocks = lines_ref.shape[1] // 2
    tiles = blocks // TILE
    size = blocks * 4
    end = channels * size
    spread(last, None, pl.ds(blocks, TILE), rows_ref, end, twist_ref, fold)
    for step in range(channels // GROUP):
        held = range(GROUP * step, GROUP * (step + 1))
        for c in held:
            lines_ref[c] = dot(lead, load(c))
        for c in held:
            for t in range(tiles):
                freqs = pl.ds(TILE * t, TILE)
                real = lines_ref[c, freqs, :]
                imag = lines_ref[c, pl.ds(blocks + TILE * t, TILE), :]
                spread(real, imag, freqs, rows_ref, c * size + 4 * TILE * t, twist_ref, fold)
        count = GROUP * size + (4 * TILE if step == channels // GROUP - 1 else 0)
        spec_ref[pl.ds(GROUP * size * step, count), :] = transform_rows(
            rows_ref, GROUP * size * step, count, line_ref
        )


def fill(flat, planes):
    blocks, channels, width = planes.shape
    rows = planes.reshape(blocks * channels, width)
    for q in range(width // 128):
        flat[q, : blocks * channels] = rows[:, 128 * q : 128 * (q + 1)]


def channel_of(flat, channel, blocks, channels):
    place = pl.ds(channel, blocks, stride=channels)
    return jnp.concatenate([flat[q, place, :] for q in range(flat.shape[0])], axis=1)


def alternating(planes):
    pairs = planes.reshape(planes.shape[0] // 2, 2, *planes.shape[1:])
    rows = jnp.sum(pairs[:, 0] - pairs[:, 1], axis=0)
    return jnp.concatenate([rows, jnp.zeros((TILE - rows.shape[0], rows.shape[1]), f32)], axis=0)


def spectrum_kernel(
    taps_ref, table_hbm, spec_hbm,
    table_ref, twist_ref, line_ref, flat, lines_ref, rows_ref, spec_ref, sems,
):
    blocks, channels, _ = taps_ref.shape
    copies = start_all([(table_hbm, table_ref)], sems)
    taps = taps_ref[...].astype(f32)
    fill(flat, taps)
    last = alternating(taps)
    for copy in copies:
        copy.wait()

    def load(c):
        value = channel_of(flat, c, blocks, channels).astype(bf16)
        return jnp.concatenate([value, value], axis=0)

    _, lead, _, fold = unpack(table_ref, blocks, line_ref, twist_ref)
    forward(load, last, lead, lines_ref, rows_ref, spec_ref, twist_ref, fold, line_ref)
    copy = pltpu.make_async_copy(spec_ref, spec_hbm.at[pl.ds(0, spec_ref.shape[0])], sems.at[1])
    copy.start()
    copy.wait()


def conv_kernel(
    gain_ref, parts_ref, spec_hbm, table_hbm, out_hbm,
    taps_spec_ref, table_ref, twist_ref, line_ref,
    flat, lines_ref, rows_ref, spec_ref, packed_ref, mixed_ref, out_ref, sems, out_sems,
):
    _, blocks, channels, width = parts_ref.shape
    lanes = flat.shape[2]
    quarters = width // lanes
    quarter = spec_ref.shape[1] // 2
    tiles = blocks // TILE
    size = blocks * 4
    half = blocks // 2
    copies = start_all([(table_hbm, table_ref), (spec_hbm.at[pl.ds(0, taps_spec_ref.shape[0])], taps_spec_ref)], sems)
    total = parts_ref[0].astype(f32) + parts_ref[1].astype(f32)
    fill(flat, total)
    last = alternating(total)
    copies[0].wait()
    lead, _, tail, fold = unpack(table_ref, blocks, line_ref, twist_ref)

    def load(c):
        high, low = split(channel_of(flat, c, blocks, channels))
        return jnp.concatenate([high, low, high], axis=0)

    forward(load, last, lead, lines_ref, rows_ref, spec_ref, twist_ref, fold, line_ref)
    copies[1].wait()

    def multiply(at, gain):
        span = pl.ds(at, 4 * TILE)
        real, imag = spec_ref[span, :quarter], spec_ref[span, quarter:]
        taps_real, taps_imag = taps_spec_ref[span, :quarter] + gain, taps_spec_ref[span, quarter:]
        put_rows(
            rows_ref, at,
            jnp.concatenate(
                [real * taps_real - imag * taps_imag, -(real * taps_imag + imag * taps_real)], axis=1
            ),
        )

    first_gain = lax.axis_index("ctx") * channels
    gain = [gain_ref[first_gain + c] for c in range(channels)]
    end = channels * size
    row = lax.broadcasted_iota(jnp.int32, (4 * TILE, quarter), 0) % TILE
    all_gains = jnp.zeros((4 * TILE, quarter), f32)
    for c in range(channels):
        all_gains = jnp.where(row == c, gain[c], all_gains)
    multiply(end, all_gains)
    spec_ref[pl.ds(end, 4 * TILE), :] = transform_rows(rows_ref, end, 4 * TILE, line_ref)
    last, _ = gather_back(spec_ref, end, pl.ds(blocks, TILE), twist_ref, fold)
    first_row = lax.broadcasted_iota(jnp.int32, (TILE, width), 0) == 0
    for step in range(channels // GROUP):
        held = range(GROUP * step, GROUP * (step + 1))
        for c in held:
            for t in range(tiles):
                multiply(c * size + 4 * TILE * t, gain[c])
        at = GROUP * size * step
        spec_ref[pl.ds(at, GROUP * size), :] = transform_rows(rows_ref, at, GROUP * size, line_ref)
        for c in held:
            for t in range(tiles):
                real, imag = gather_back(
                    spec_ref, c * size + 4 * TILE * t, pl.ds(TILE * t, TILE), twist_ref, fold
                )
                if t == 0:
                    imag = jnp.where(first_row, last[c : c + 1], imag)
                for at, part in ((TILE * t, real), (blocks + TILE * t, imag)):
                    high, low = split(part)
                    packed_ref[c, pl.ds(at, TILE), :] = high
                    packed_ref[c, pl.ds(2 * blocks + at, TILE), :] = low
            both = dot(tail, packed_ref[c])
            value = both[:blocks] + both[blocks:]
            for q in range(quarters):
                mixed_ref[q, pl.ds(c, blocks, stride=channels), :] = value[:, lanes * q : lanes * (q + 1)]
    stores = []
    for i in range(2):
        span = pl.ds(half * i, half)
        for q in range(quarters):
            result = mixed_ref[q, pl.ds(half * channels * i, half * channels), :].astype(bf16)
            out_ref[span, :, lanes * q : lanes * (q + 1)] = result.reshape(half, channels, lanes)
        for k in range(2):
            stores.append(
                pltpu.make_async_copy(out_ref.at[span], out_hbm.at[k, span], out_sems.at[2 * i + k])
            )
            stores[-1].start()
    for copy in stores:
        copy.wait()


def prepare_kernel(
    taps_hbm, weight_hbm, out_hbm, piece_hbm, taps_ref, out_ref, piece_ref, sems, out_sems
):
    steps = sems.shape[0] - 1
    size = taps_ref.shape[1] // steps
    spans = [pl.ds(i * size, size) for i in range(steps)]
    loads = start_all(
        [(taps_hbm.at[:, s], taps_ref.at[:, s]) for s in spans]
        + [(piece_source(weight_hbm, piece_hbm, 0), piece_ref)],
        sems,
    )
    stores = []
    for i in range(steps):
        loads[i].wait()
        at = slice(i * size, (i + 1) * size)
        out_ref[at, :] = taps_ref[:, at].astype(bf16).T
        stores.append(pltpu.make_async_copy(out_ref.at[spans[i]], out_hbm.at[spans[i]], out_sems.at[i]))
        stores[-1].start()
    loads[steps].wait()
    stores.append(pltpu.make_async_copy(piece_ref, piece_hbm, out_sems.at[steps]))
    stores[-1].start()
    for store in stores:
        store.wait()


def piece_source(weight_hbm, piece_ref, chosen):
    group, core, x, z = where()
    size, columns = piece_ref.shape
    at = pl.ds(pl.multiple_of((1 - group) * columns, columns), columns)
    start = (core * PIECES + held_pieces(x, z)[chosen]) * size
    return weight_hbm.at[pl.ds(pl.multiple_of(start, size), size), at]


def last_piece_kernel(weight_hbm, after_ref, out_hbm, piece_ref, sems):
    source = piece_source(weight_hbm, out_hbm, PIECES - 1)
    for a, b, sem in ((source, piece_ref, sems.at[0]), (piece_ref, out_hbm, sems.at[1])):
        copy = pltpu.make_async_copy(a, b, sem)
        copy.start()
        copy.wait()


def fence_kernel(value_ref, after_ref, out_ref):
    pass


def project_kernel(
    tokens_hbm, weight_hbm, out_hbm, tokens_ref, weight_ref, total, out_ref,
    token_sems, weight_sems, out_sems,
):
    features = tokens_ref.shape[1]
    width = weight_ref.shape[1]
    steps = features // CHUNK
    parts = 4
    loads = []
    for i in range(steps):
        at = pl.ds(i * CHUNK, CHUNK)
        pair = (
            pltpu.make_async_copy(tokens_hbm.at[:, at], tokens_ref.at[:, at], token_sems.at[i]),
            pltpu.make_async_copy(weight_hbm.at[at], weight_ref.at[at], weight_sems.at[i]),
        )
        for copy in pair:
            copy.start()
        loads.append(pair)
    stores = []
    for i in range(steps):
        for copy in loads[i]:
            copy.wait()
        at = slice(i * CHUNK, (i + 1) * CHUNK)
        for c in range(parts):
            cols = slice(c * width // parts, (c + 1) * width // parts)
            term = dot(tokens_ref[:, at], weight_ref[at, cols])
            if i == 0:
                total[:, cols] = term
            elif i < steps - 1:
                total[:, cols] += term
            else:
                out_ref[cols, :] = (total[:, cols] + term).astype(bf16).T
                rows = pl.ds(c * width // parts, width // parts)
                store = pltpu.make_async_copy(out_ref.at[rows], out_hbm.at[rows], out_sems.at[c])
                store.start()
                stores.append(store)
    for store in stores:
        store.wait()


def weights_kernel(own_hbm, *rest):
    pieces, (out_hbm, held_ref, sems, out_sems) = rest[:-4], rest[-4:]
    rows = own_hbm.shape[0]
    blocks, _, columns = out_hbm.shape
    group = where()[0]
    at = pl.ds(pl.multiple_of(group * (blocks * columns), columns), blocks * columns)
    pairs = [(own_hbm.at[:, at], held_ref.at[pl.ds(0, rows)])]
    for piece in pieces:
        size = piece.shape[0]
        pairs.append((piece, held_ref.at[pl.ds(rows, size)]))
        rows += size
    for copy in start_all(pairs, sems):
        copy.wait()
    stores = start_all(
        [(held_ref.at[:, pl.ds(b * columns, columns)], out_hbm.at[b]) for b in range(blocks)],
        out_sems,
    )
    for copy in stores:
        copy.wait()


def out_kernel(mixed_ref, weight_hbm, out_hbm, turned, weight_ref, out_ref, sems, out_sems):
    steps, _, columns = weight_ref.shape
    loads = start_all([(weight_hbm.at[i], weight_ref.at[i]) for i in range(steps)], sems)
    group, core, x, z = where()
    width = mixed_ref.shape[0]
    rows = width // 2
    size = rows // (2 * PIECES)
    own = mixed_ref[pl.ds(pl.multiple_of(group * rows, rows), rows), :]
    turned[:, :rows] = own.T
    pieces = []
    for half in (core, 1 - core):
        for k in held_pieces(x, z):
            start = (1 - group) * rows + (half * PIECES + k) * size
            pieces.append(mixed_ref[pl.ds(pl.multiple_of(start, size), size), :])
    turned[:, rows:] = jnp.concatenate(pieces, axis=0).T
    stores = []
    for i in range(steps):
        loads[i].wait()
        at = slice(i * columns, (i + 1) * columns)
        if i < steps - 1:
            out_ref[:, at] = dot(turned[...], weight_ref[i]).astype(bf16)
            if i % 2:
                stores.append((slice(None), pl.ds((i - 1) * columns, 2 * columns)))
            elif i == steps - 2:
                stores.append((slice(None), pl.ds(i * columns, columns)))
            else:
                continue
            start_store(out_ref, out_hbm, out_sems, stores)
            continue
        count = turned.shape[0] // LAST_PARTS
        for r in range(LAST_PARTS):
            part = slice(r * count, (r + 1) * count)
            out_ref[part, at] = dot(turned[part, :], weight_ref[i]).astype(bf16)
            stores.append((pl.ds(r * count, count), pl.ds(i * columns, columns)))
            start_store(out_ref, out_hbm, out_sems, stores)
    for i, span in enumerate(stores):
        pltpu.make_async_copy(out_ref.at[span], out_hbm.at[span], out_sems.at[i]).wait()


def start_store(out_ref, out_hbm, out_sems, stores):
    span = stores[-1]
    pltpu.make_async_copy(out_ref.at[span], out_hbm.at[span], out_sems.at[len(stores) - 1]).start()


def vmem(limit):
    return pltpu.CompilerParams(vmem_limit_bytes=limit * MIB)


def cost(flops, size):
    return pl.CostEstimate(flops=flops, bytes_accessed=size, transcendentals=0)


ANY = pl.BlockSpec(memory_space=pl.ANY)
SMEM = pl.BlockSpec(memory_space=pltpu.SMEM)
VMEM = pl.BlockSpec(memory_space=pltpu.VMEM)


def partners(move):
    def place(y, x, z, core):
        return (((y % 2 * 4 + x) * 4 + z) * 2 + core) * 2 + y // 2

    spots = [(y, x, z, c) for y in range(4) for x in range(4) for z in range(4) for c in range(2)]
    return [(place(*spot), place(*move(*spot))) for spot in spots]


def shards(tokens, in_weight, filter_taps, skip_gain, out_weight):
    ctx, ch = lax.axis_size("ctx"), lax.axis_size("ch")
    devices = ctx * ch
    position, features = tokens.shape
    width = in_weight.shape[1]
    channels = width // devices
    rows = out_weight.shape[0]
    table = jnp.asarray(tables(ctx, position))
    lanes = 128
    quarters = position // lanes
    both = ("ctx", "ch")
    across = partners(lambda y, x, z, c: (3 - y, x, z, c))
    other_core = partners(lambda y, x, z, c: (y, x, z, 1 - c))
    along_x = partners(lambda y, x, z, c: (y, x ^ 1, z, c))
    along_z = partners(lambda y, x, z, c: (y, x, z ^ 1, c))
    size = rows // (2 * PIECES)

    piece = jax.ShapeDtypeStruct((size, features), bf16)
    taps, first_piece = pl.pallas_call(
        prepare_kernel,
        in_specs=[ANY] * 2,
        out_specs=[ANY] * 2,
        out_shape=[jax.ShapeDtypeStruct((width // ch, position), bf16), piece],
        scratch_shapes=[
            pltpu.VMEM((position, width // ch), f32),
            pltpu.VMEM((width // ch, position), bf16),
            pltpu.VMEM(piece.shape, bf16),
            pltpu.SemaphoreType.DMA((3,)),
            pltpu.SemaphoreType.DMA((3,)),
        ],
        compiler_params=vmem(60),
        cost_estimate=cost(0, 2 * MIB),
    )(filter_taps, out_weight)
    mine = lax.ppermute(first_piece, both, across)
    taps = lax.all_to_all(
        taps.reshape(ctx, channels, position), "ctx", split_axis=0, concat_axis=0, tiled=True
    )

    partial_value = pl.pallas_call(
        project_kernel,
        in_specs=[ANY] * 2,
        out_specs=ANY,
        out_shape=jax.ShapeDtypeStruct((width, position), bf16),
        scratch_shapes=[
            pltpu.VMEM((position, features), bf16),
            pltpu.VMEM((features, width), bf16),
            pltpu.VMEM((position, width), f32),
            pltpu.VMEM((width, position), bf16),
            pltpu.SemaphoreType.DMA((features // CHUNK,)),
            pltpu.SemaphoreType.DMA((features // CHUNK,)),
            pltpu.SemaphoreType.DMA((4,)),
        ],
        compiler_params=vmem(60),
        cost_estimate=cost(2 * position * features * width, 14 * MIB),
    )(tokens, in_weight)
    partial_value = pl.pallas_call(
        fence_kernel,
        in_specs=[ANY] * 2,
        out_specs=ANY,
        out_shape=jax.ShapeDtypeStruct((width, position), bf16),
        input_output_aliases={0: 0},
        compiler_params=vmem(60),
        cost_estimate=cost(0, 0),
    )(partial_value, mine)
    parts = lax.all_to_all(
        partial_value.reshape(devices, channels, position),
        ("ch", "ctx"), split_axis=0, concat_axis=0, tiled=True,
    ).reshape(ch, ctx, channels, position)

    by_x = lax.ppermute(mine, both, along_x)
    by_z = lax.ppermute(mine, both, along_z)
    last_piece = pl.pallas_call(
        last_piece_kernel,
        in_specs=[ANY] * 2,
        out_specs=ANY,
        out_shape=piece,
        scratch_shapes=[pltpu.VMEM(piece.shape, bf16), pltpu.SemaphoreType.DMA((2,))],
        compiler_params=vmem(60),
        cost_estimate=cost(0, MIB),
    )(out_weight, partial_value)
    last = lax.ppermute(last_piece, both, across)
    pieces = [mine, by_z, by_x, last]
    pieces = pieces + [lax.ppermute(p, both, other_core) for p in pieces]

    lines = channels * 4 * ctx + 4 * TILE
    flat = (quarters, ctx * channels, lanes)
    held = [
        pltpu.VMEM(table.shape, f32),
        pltpu.VMEM((2, ctx + TILE, position), f32),
        pltpu.VMEM((3 * (position // 2), position // 2), bf16),
        pltpu.VMEM(flat, f32),
        pltpu.VMEM((channels, 2 * ctx, position), f32),
        pltpu.VMEM((lines, position), bf16),
        pltpu.VMEM((lines, position // 2), f32),
    ]
    spec = pl.pallas_call(
        spectrum_kernel,
        in_specs=[VMEM, ANY],
        out_specs=ANY,
        out_shape=jax.ShapeDtypeStruct((SPARE * lines, position // 2), f32),
        scratch_shapes=held + [pltpu.SemaphoreType.DMA((2,))],
        compiler_params=vmem(58),
        cost_estimate=cost(4 * 10**9, 4 * MIB),
    )(taps, table)
    mixed = pl.pallas_call(
        conv_kernel,
        in_specs=[SMEM, VMEM] + [ANY] * 2,
        out_specs=ANY,
        out_shape=jax.ShapeDtypeStruct((ch, ctx, channels, position), bf16),
        scratch_shapes=[
            pltpu.VMEM((lines, position // 2), f32),
            *held,
            pltpu.VMEM((channels, 4 * ctx, position), bf16),
            pltpu.VMEM(flat, f32),
            pltpu.VMEM((ctx, channels, position), bf16),
            pltpu.SemaphoreType.DMA((2,)),
            pltpu.SemaphoreType.DMA((4,)),
        ],
        compiler_params=vmem(40),
        cost_estimate=cost(8 * 10**9, 6 * MIB),
    )(skip_gain, parts, spec, table)

    mixed = lax.all_to_all(
        mixed.reshape(devices, channels, position),
        ("ch", "ctx"), split_axis=0, concat_axis=0, tiled=True,
    ).reshape(width, position)

    steps = features // 1024
    weights = pl.pallas_call(
        weights_kernel,
        in_specs=[ANY] * (1 + len(pieces)),
        out_specs=ANY,
        out_shape=jax.ShapeDtypeStruct((steps, width, features // steps), bf16),
        scratch_shapes=[
            pltpu.VMEM((width, features), bf16),
            pltpu.SemaphoreType.DMA((1 + len(pieces),)),
            pltpu.SemaphoreType.DMA((steps,)),
        ],
        compiler_params=vmem(60),
        cost_estimate=cost(0, 16 * MIB),
    )(out_weight, *pieces)

    return pl.pallas_call(
        out_kernel,
        in_specs=[VMEM, ANY],
        out_specs=ANY,
        out_shape=jax.ShapeDtypeStruct((position, features), bf16),
        scratch_shapes=[
            pltpu.VMEM((position, width), bf16),
            pltpu.VMEM((steps, width, features // steps), bf16),
            pltpu.VMEM((position, features), bf16),
            pltpu.SemaphoreType.DMA((steps,)),
            pltpu.SemaphoreType.DMA((steps + LAST_PARTS,)),
        ],
        compiler_params=vmem(48),
        cost_estimate=cost(2 * position * features * width, 13 * MIB),
    )(mixed, weights)


def solution(mesh):
    return jax.shard_map(
        shards,
        mesh=mesh,
        in_specs=(P("ctx", "ch"), P("ch", None), P("ctx", "ch"), P("ch"), P("ch", None)),
        out_specs=P("ctx", "ch"),
        check_vma=False,
    )
```

```python
import numpy as np
import ml_dtypes
import jax
import jax.numpy as jnp
from jax import lax
from jax.experimental import pallas as pl
from jax.experimental.pallas import tpu as pltpu
from jax.sharding import PartitionSpec as P

bf16 = jnp.bfloat16
f32 = jnp.float32
MIB = 1024 * 1024
TILE = 16
GROUP = 4
CHUNK = 512
SPARE = 12
LAST_PARTS = 4
PIECES = 4


def split_table(table):
    high = table.astype(ml_dtypes.bfloat16)
    low = (table - high.astype(np.float64)).astype(ml_dtypes.bfloat16)
    return high, low


def tables(blocks, width):
    period = 2 * blocks * width
    quarter = width // 4
    freq = np.arange(blocks)[:, None]
    angle = 2.0 * np.pi * (freq * np.arange(blocks)[None, :] % (2 * blocks)) / (2 * blocks)
    lead_high, lead_low = split_table(np.concatenate([np.cos(angle), -np.sin(angle)], axis=0))
    weight = np.where(freq == 0, 1.0, 2.0) / period
    cosines, sines = np.cos(angle) * weight, np.sin(angle) * weight
    sines[0] = (1.0 - 2.0 * (np.arange(blocks) % 2)) / period
    tail_high, tail_low = split_table(np.concatenate([cosines, sines], axis=0).T)
    turned = np.concatenate([freq, np.full((TILE, 1), blocks)])
    turn = 2.0 * np.pi * turned * np.arange(width)[None, :] / period
    fold = 2.0 * np.pi * np.arange(4)[:, None] * np.arange(quarter)[None, :] / width
    index = np.arange(quarter)
    line = 2.0 * np.pi * (index[:, None] * index[None, :] % quarter) / quarter
    cos, sin = np.cos(line), np.sin(line)
    line_high, line_low = split_table(np.block([[cos, -sin], [sin, cos]]))
    parts = [
        line_high,
        line_low,
        np.concatenate([lead_high, lead_high, lead_low], axis=1),
        np.concatenate([lead_high, lead_low], axis=1),
        np.block([[tail_high, tail_high], [tail_low, np.zeros_like(tail_low)]]),
        *np.split(np.cos(turn), 2, axis=1),
        *np.split(np.sin(turn), 2, axis=1),
        np.concatenate([np.cos(fold), np.sin(fold)]),
    ]
    columns = line_high.shape[1]
    return np.concatenate(
        [np.pad(p.astype(np.float32), ((0, 0), (0, columns - p.shape[1]))) for p in parts]
    )


def unpack(table_ref, blocks, line_ref):
    columns = line_ref.shape[1]
    line_ref[:columns] = table_ref[:columns, :].astype(bf16)
    line_ref[columns:] = table_ref[: 2 * columns, :].astype(bf16)
    at = 2 * columns
    leads = []
    for use in (3 * blocks, 2 * blocks, 4 * blocks):
        leads.append(table_ref[at : at + 2 * blocks, :use].astype(bf16))
        at += 2 * blocks
    rows = blocks + TILE
    quarter = columns // 2

    def twist(first, p):
        lanes = slice(quarter * (p % 2), quarter * (p % 2 + 1))
        start = at + p // 2 * rows + first
        return [table_ref[start + 2 * i * rows : start + 2 * i * rows + TILE, lanes] for i in range(2)]

    end = at + 4 * rows
    return (*leads, table_ref[end : end + 8, :quarter], twist)


def dot(a, b):
    return jnp.dot(a, b, preferred_element_type=f32)


def split(a):
    high = a.astype(bf16)
    return high, (a - high.astype(f32)).astype(bf16)


def turn_back(real, imag, cos, sin):
    return real * cos + imag * sin, imag * cos - real * sin


def butterfly(parts):
    (ar, ai), (br, bi), (cr, ci), (dr, di) = parts
    sr, si, er, ei = ar + cr, ai + ci, ar - cr, ai - ci
    tr, ti, fr, fi = br + dr, bi + di, br - dr, bi - di
    return [(sr + tr, si + ti), (er + fi, ei - fr), (sr - tr, si - ti), (er - fi, ei + fr)]


def put_rows(rows_ref, at, value):
    high, low = split(value)
    size = value.shape[1]
    span = pl.ds(at, value.shape[0])
    rows_ref[span, :size] = high
    rows_ref[span, size : 2 * size] = low


def transform_rows(rows_ref, at, count, line_ref):
    size = line_ref.shape[1]
    span = pl.ds(at, count)
    both = dot(rows_ref[span, :], line_ref[: 2 * size, :])
    return both + dot(rows_ref[span, :size], line_ref[2 * size :, :])


def spread(real, imag, first, rows_ref, at, twist, fold):
    quarter = real.shape[1] // 4
    parts = []
    for p in range(4):
        lanes = slice(quarter * p, quarter * (p + 1))
        cos, sin = twist(first, p)
        if imag is None:
            parts.append((real[:, lanes] * cos, -real[:, lanes] * sin))
        else:
            parts.append(turn_back(real[:, lanes], imag[:, lanes], cos, sin))
    for r, (a, b) in enumerate(butterfly(parts)):
        if r:
            a, b = turn_back(a, b, fold[r : r + 1], fold[r + 4 : r + 5])
        put_rows(rows_ref, at + TILE * r, jnp.concatenate([a, b], axis=1))


def gather_back(back_ref, at, first, twist, fold):
    quarter = back_ref.shape[1] // 2
    got = []
    for r in range(4):
        span = pl.ds(at + TILE * r, TILE)
        a, b = back_ref[span, :quarter], back_ref[span, quarter:]
        if r:
            a, b = turn_back(a, b, fold[r : r + 1], fold[r + 4 : r + 5])
        got.append((a, b))
    reals, imags = [], []
    for p, (a, b) in enumerate(butterfly(got)):
        a, b = turn_back(a, b, *twist(first, p))
        reals.append(a)
        imags.append(b)
    return jnp.concatenate(reals, axis=1), jnp.concatenate(imags, axis=1)


def where():
    here = lax.axis_index("ctx")
    return lax.axis_index("ch"), here & 1, here >> 3 & 3, here >> 1 & 3


def held_pieces(x, z):
    first = (x & 1) * 2 + (z & 1)
    return [first ^ flip for flip in range(PIECES)]


def start_all(pairs, sems):
    copies = [pltpu.make_async_copy(a, b, sems.at[i]) for i, (a, b) in enumerate(pairs)]
    for copy in copies:
        copy.start()
    return copies


def forward(load, last, lead, lines_ref, rows_ref, spec_ref, twist, fold, line_ref):
    channels = lines_ref.shape[0]
    blocks = lines_ref.shape[1] // 2
    tiles = blocks // TILE
    size = blocks * 4
    end = channels * size
    spread(last, None, blocks, rows_ref, end, twist, fold)
    for step in range(channels // GROUP):
        held = range(GROUP * step, GROUP * (step + 1))
        for c in held:
            lines_ref[c] = dot(lead, load(c))
        for c in held:
            for t in range(tiles):
                real = lines_ref[c, pl.ds(TILE * t, TILE), :]
                imag = lines_ref[c, pl.ds(blocks + TILE * t, TILE), :]
                spread(real, imag, TILE * t, rows_ref, c * size + 4 * TILE * t, twist, fold)
        count = GROUP * size + (4 * TILE if step == channels // GROUP - 1 else 0)
        spec_ref[pl.ds(GROUP * size * step, count), :] = transform_rows(
            rows_ref, GROUP * size * step, count, line_ref
        )


def fill(flat, planes):
    blocks, channels, width = planes.shape
    rows = planes.reshape(blocks * channels, width)
    for q in range(width // 128):
        flat[q, : blocks * channels] = rows[:, 128 * q : 128 * (q + 1)]


def channel_of(flat, channel, blocks, channels):
    place = pl.ds(channel, blocks, stride=channels)
    return jnp.concatenate([flat[q, place, :] for q in range(flat.shape[0])], axis=1)


def alternating(planes):
    pairs = planes.reshape(planes.shape[0] // 2, 2, *planes.shape[1:])
    rows = jnp.sum(pairs[:, 0] - pairs[:, 1], axis=0)
    return jnp.concatenate([rows, jnp.zeros((TILE - rows.shape[0], rows.shape[1]), f32)], axis=0)


def spectrum_kernel(
    taps_ref, table_hbm, spec_hbm,
    table_ref, line_ref, flat, lines_ref, rows_ref, spec_ref, sems,
):
    blocks, channels, _ = taps_ref.shape
    copies = start_all([(table_hbm, table_ref)], sems)
    taps = taps_ref[...].astype(f32)
    fill(flat, taps)
    last = alternating(taps)
    for copy in copies:
        copy.wait()

    def load(c):
        value = channel_of(flat, c, blocks, channels).astype(bf16)
        return jnp.concatenate([value, value], axis=0)

    _, lead, _, fold, twist = unpack(table_ref, blocks, line_ref)
    forward(load, last, lead, lines_ref, rows_ref, spec_ref, twist, fold, line_ref)
    copy = pltpu.make_async_copy(spec_ref, spec_hbm.at[pl.ds(0, spec_ref.shape[0])], sems.at[1])
    copy.start()
    copy.wait()


def conv_kernel(
    gain_ref, parts_ref, spec_hbm, table_ref, out_hbm,
    taps_spec_ref, line_ref,
    flat, lines_ref, rows_ref, spec_ref, packed_ref, mixed_ref, out_ref, sems, out_sems,
):
    _, blocks, channels, width = parts_ref.shape
    lanes = flat.shape[2]
    quarters = width // lanes
    quarter = spec_ref.shape[1] // 2
    tiles = blocks // TILE
    size = blocks * 4
    half = blocks // 2
    copies = start_all([(spec_hbm.at[pl.ds(0, taps_spec_ref.shape[0])], taps_spec_ref)], sems)
    total = parts_ref[0].astype(f32) + parts_ref[1].astype(f32)
    fill(flat, total)
    last = alternating(total)
    lead, _, tail, fold, twist = unpack(table_ref, blocks, line_ref)

    def load(c):
        high, low = split(channel_of(flat, c, blocks, channels))
        return jnp.concatenate([high, low, high], axis=0)

    forward(load, last, lead, lines_ref, rows_ref, spec_ref, twist, fold, line_ref)
    copies[0].wait()

    def multiply(at, gain):
        span = pl.ds(at, 4 * TILE)
        real, imag = spec_ref[span, :quarter], spec_ref[span, quarter:]
        taps_real, taps_imag = taps_spec_ref[span, :quarter] + gain, taps_spec_ref[span, quarter:]
        put_rows(
            rows_ref, at,
            jnp.concatenate(
                [real * taps_real - imag * taps_imag, -(real * taps_imag + imag * taps_real)], axis=1
            ),
        )

    first_gain = lax.axis_index("ctx") * channels
    gain = [gain_ref[first_gain + c] for c in range(channels)]
    end = channels * size
    row = lax.broadcasted_iota(jnp.int32, (4 * TILE, quarter), 0) % TILE
    all_gains = jnp.zeros((4 * TILE, quarter), f32)
    for c in range(channels):
        all_gains = jnp.where(row == c, gain[c], all_gains)
    multiply(end, all_gains)
    spec_ref[pl.ds(end, 4 * TILE), :] = transform_rows(rows_ref, end, 4 * TILE, line_ref)
    last, _ = gather_back(spec_ref, end, blocks, twist, fold)
    first_row = lax.broadcasted_iota(jnp.int32, (TILE, width), 0) == 0
    for step in range(channels // GROUP):
        held = range(GROUP * step, GROUP * (step + 1))
        for c in held:
            for t in range(tiles):
                multiply(c * size + 4 * TILE * t, gain[c])
        at = GROUP * size * step
        spec_ref[pl.ds(at, GROUP * size), :] = transform_rows(rows_ref, at, GROUP * size, line_ref)
        for c in held:
            for t in range(tiles):
                real, imag = gather_back(spec_ref, c * size + 4 * TILE * t, TILE * t, twist, fold)
                if t == 0:
                    imag = jnp.where(first_row, last[c : c + 1], imag)
                for at, part in ((TILE * t, real), (blocks + TILE * t, imag)):
                    high, low = split(part)
                    packed_ref[c, pl.ds(at, TILE), :] = high
                    packed_ref[c, pl.ds(2 * blocks + at, TILE), :] = low
    for c in range(channels):
        both = dot(tail, packed_ref[c])
        value = both[:blocks] + both[blocks:]
        for q in range(quarters):
            mixed_ref[q, pl.ds(c, blocks, stride=channels), :] = value[:, lanes * q : lanes * (q + 1)]
    stores = []
    for i in range(2):
        span = pl.ds(half * i, half)
        for q in range(quarters):
            result = mixed_ref[q, pl.ds(half * channels * i, half * channels), :].astype(bf16)
            out_ref[span, :, lanes * q : lanes * (q + 1)] = result.reshape(half, channels, lanes)
        for k in range(2):
            stores.append(
                pltpu.make_async_copy(out_ref.at[span], out_hbm.at[k, span], out_sems.at[2 * i + k])
            )
            stores[-1].start()
    for copy in stores:
        copy.wait()


def prepare_kernel(
    taps_hbm, weight_hbm, out_hbm, piece_hbm, taps_ref, out_ref, piece_ref, sems, out_sems
):
    steps = sems.shape[0] - 1
    size = taps_ref.shape[0] // steps
    spans = [pl.ds(i * size, size) for i in range(steps)]
    loads = start_all(
        [(taps_hbm.at[s], taps_ref.at[s]) for s in spans]
        + [(piece_source(weight_hbm, piece_hbm, 0), piece_ref)],
        sems,
    )
    for load in loads[:steps]:
        load.wait()
    stores = []
    for i, span in enumerate(spans):
        out_ref[span, :] = taps_ref[:, i * size : (i + 1) * size].astype(bf16).T
        stores.append(pltpu.make_async_copy(out_ref.at[span], out_hbm.at[span], out_sems.at[i]))
        stores[-1].start()
    loads[steps].wait()
    stores.append(pltpu.make_async_copy(piece_ref, piece_hbm, out_sems.at[steps]))
    stores[-1].start()
    for store in stores:
        store.wait()


def piece_source(weight_hbm, piece_ref, chosen):
    group, core, x, z = where()
    size, columns = piece_ref.shape
    at = pl.ds(pl.multiple_of((1 - group) * columns, columns), columns)
    start = (core * PIECES + held_pieces(x, z)[chosen]) * size
    return weight_hbm.at[pl.ds(pl.multiple_of(start, size), size), at]


def last_piece_kernel(weight_hbm, after_ref, out_hbm, piece_ref, sems):
    source = piece_source(weight_hbm, out_hbm, PIECES - 1)
    for a, b, sem in ((source, piece_ref, sems.at[0]), (piece_ref, out_hbm, sems.at[1])):
        copy = pltpu.make_async_copy(a, b, sem)
        copy.start()
        copy.wait()


def fence_kernel(value_ref, after_ref, out_ref):
    pass


def project_kernel(
    tokens_hbm, weight_hbm, out_hbm, tokens_ref, weight_ref, total, out_ref,
    token_sems, weight_sems, out_sems,
):
    features = tokens_ref.shape[1]
    width = weight_ref.shape[1]
    steps = features // CHUNK
    parts = 4
    loads = []
    for i in range(steps):
        at = pl.ds(i * CHUNK, CHUNK)
        pair = (
            pltpu.make_async_copy(tokens_hbm.at[:, at], tokens_ref.at[:, at], token_sems.at[i]),
            pltpu.make_async_copy(weight_hbm.at[at], weight_ref.at[at], weight_sems.at[i]),
        )
        for copy in pair:
            copy.start()
        loads.append(pair)
    stores = []
    for i in range(steps):
        for copy in loads[i]:
            copy.wait()
        at = slice(i * CHUNK, (i + 1) * CHUNK)
        for c in range(parts):
            cols = slice(c * width // parts, (c + 1) * width // parts)
            term = dot(tokens_ref[:, at], weight_ref[at, cols])
            if i == 0:
                total[:, cols] = term
            elif i < steps - 1:
                total[:, cols] += term
            else:
                out_ref[cols, :] = (total[:, cols] + term).astype(bf16).T
                rows = pl.ds(c * width // parts, width // parts)
                store = pltpu.make_async_copy(out_ref.at[rows], out_hbm.at[rows], out_sems.at[c])
                store.start()
                stores.append(store)
    for store in stores:
        store.wait()


def weights_kernel(own_hbm, *rest):
    pieces, (out_hbm, held_ref, sems, out_sems) = rest[:-4], rest[-4:]
    rows = own_hbm.shape[0]
    blocks, _, columns = out_hbm.shape
    group = where()[0]
    at = pl.ds(pl.multiple_of(group * (blocks * columns), columns), blocks * columns)
    pairs = [(own_hbm.at[:, at], held_ref.at[pl.ds(0, rows)])]
    for piece in pieces:
        size = piece.shape[0]
        pairs.append((piece, held_ref.at[pl.ds(rows, size)]))
        rows += size
    for copy in start_all(pairs, sems):
        copy.wait()
    stores = start_all(
        [(held_ref.at[:, pl.ds(b * columns, columns)], out_hbm.at[b]) for b in range(blocks)],
        out_sems,
    )
    for copy in stores:
        copy.wait()


def out_kernel(mixed_ref, weight_hbm, out_hbm, turned, weight_ref, out_ref, sems, out_sems):
    steps, _, columns = weight_ref.shape
    width = mixed_ref.shape[0]
    rows = width // 2
    parts = [(0, pl.ds(0, rows)), (0, pl.ds(rows, rows)), *range(1, steps)]
    loads = start_all([(weight_hbm.at[i], weight_ref.at[i]) for i in parts], sems)
    group, core, x, z = where()
    size = rows // (2 * PIECES)
    own = mixed_ref[pl.ds(pl.multiple_of(group * rows, rows), rows), :]
    turned[:, :rows] = own.T
    pieces = []
    for half in (core, 1 - core):
        for k in held_pieces(x, z):
            start = (1 - group) * rows + (half * PIECES + k) * size
            pieces.append(mixed_ref[pl.ds(pl.multiple_of(start, size), size), :])
    turned[:, rows:] = jnp.concatenate(pieces, axis=0).T
    loads[0].wait()
    own_part = dot(turned[:, :rows], weight_ref[0, :rows])
    loads[1].wait()
    out_ref[:, :columns] = (own_part + dot(turned[:, rows:], weight_ref[0, rows:])).astype(bf16)
    stores = []
    for i in range(1, steps):
        loads[i + 1].wait()
        at = slice(i * columns, (i + 1) * columns)
        if i < steps - 1:
            out_ref[:, at] = dot(turned[...], weight_ref[i]).astype(bf16)
            if i % 2:
                stores.append((slice(None), pl.ds((i - 1) * columns, 2 * columns)))
            elif i == steps - 2:
                stores.append((slice(None), pl.ds(i * columns, columns)))
            else:
                continue
            start_store(out_ref, out_hbm, out_sems, stores)
            continue
        count = turned.shape[0] // LAST_PARTS
        for r in range(LAST_PARTS):
            part = slice(r * count, (r + 1) * count)
            out_ref[part, at] = dot(turned[part, :], weight_ref[i]).astype(bf16)
            stores.append((pl.ds(r * count, count), pl.ds(i * columns, columns)))
            start_store(out_ref, out_hbm, out_sems, stores)
    for i, span in enumerate(stores):
        pltpu.make_async_copy(out_ref.at[span], out_hbm.at[span], out_sems.at[i]).wait()


def start_store(out_ref, out_hbm, out_sems, stores):
    span = stores[-1]
    pltpu.make_async_copy(out_ref.at[span], out_hbm.at[span], out_sems.at[len(stores) - 1]).start()


def vmem(limit):
    return pltpu.CompilerParams(vmem_limit_bytes=limit * MIB)


def cost(flops, size):
    return pl.CostEstimate(flops=flops, bytes_accessed=size, transcendentals=0)


ANY = pl.BlockSpec(memory_space=pl.ANY)
SMEM = pl.BlockSpec(memory_space=pltpu.SMEM)
VMEM = pl.BlockSpec(memory_space=pltpu.VMEM)


def partners(move):
    def place(y, x, z, core):
        return (((y % 2 * 4 + x) * 4 + z) * 2 + core) * 2 + y // 2

    spots = [(y, x, z, c) for y in range(4) for x in range(4) for z in range(4) for c in range(2)]
    return [(place(*spot), place(*move(*spot))) for spot in spots]


def shards(tokens, in_weight, filter_taps, skip_gain, out_weight):
    ctx, ch = lax.axis_size("ctx"), lax.axis_size("ch")
    devices = ctx * ch
    position, features = tokens.shape
    width = in_weight.shape[1]
    channels = width // devices
    rows = out_weight.shape[0]
    table = jnp.asarray(tables(ctx, position))
    lanes = 128
    quarters = position // lanes
    both = ("ctx", "ch")
    across = partners(lambda y, x, z, c: (3 - y, x, z, c))
    other_core = partners(lambda y, x, z, c: (y, x, z, 1 - c))
    along_x = partners(lambda y, x, z, c: (y, x ^ 1, z, c))
    along_z = partners(lambda y, x, z, c: (y, x, z ^ 1, c))
    size = rows // (2 * PIECES)

    piece = jax.ShapeDtypeStruct((size, features), bf16)
    taps, first_piece = pl.pallas_call(
        prepare_kernel,
        in_specs=[ANY] * 2,
        out_specs=[ANY] * 2,
        out_shape=[jax.ShapeDtypeStruct((width // ch, position), bf16), piece],
        scratch_shapes=[
            pltpu.VMEM((position, width // ch), f32),
            pltpu.VMEM((width // ch, position), bf16),
            pltpu.VMEM(piece.shape, bf16),
            pltpu.SemaphoreType.DMA((5,)),
            pltpu.SemaphoreType.DMA((5,)),
        ],
        compiler_params=vmem(60),
        cost_estimate=cost(0, 2 * MIB),
    )(filter_taps, out_weight)
    mine = lax.ppermute(first_piece, both, across)
    taps = lax.all_to_all(
        taps.reshape(ctx, channels, position), "ctx", split_axis=0, concat_axis=0, tiled=True
    )

    partial_value = pl.pallas_call(
        project_kernel,
        in_specs=[ANY] * 2,
        out_specs=ANY,
        out_shape=jax.ShapeDtypeStruct((width, position), bf16),
        scratch_shapes=[
            pltpu.VMEM((position, features), bf16),
            pltpu.VMEM((features, width), bf16),
            pltpu.VMEM((position, width), f32),
            pltpu.VMEM((width, position), bf16),
            pltpu.SemaphoreType.DMA((features // CHUNK,)),
            pltpu.SemaphoreType.DMA((features // CHUNK,)),
            pltpu.SemaphoreType.DMA((4,)),
        ],
        compiler_params=vmem(60),
        cost_estimate=cost(2 * position * features * width, 14 * MIB),
    )(tokens, in_weight)
    partial_value = pl.pallas_call(
        fence_kernel,
        in_specs=[ANY] * 2,
        out_specs=ANY,
        out_shape=jax.ShapeDtypeStruct((width, position), bf16),
        input_output_aliases={0: 0},
        compiler_params=vmem(60),
        cost_estimate=cost(0, 0),
    )(partial_value, mine)
    parts = lax.all_to_all(
        partial_value.reshape(devices, channels, position),
        ("ch", "ctx"), split_axis=0, concat_axis=0, tiled=True,
    ).reshape(ch, ctx, channels, position)

    by_x = lax.ppermute(mine, both, along_x)
    by_z = lax.ppermute(mine, both, along_z)
    last_piece = pl.pallas_call(
        last_piece_kernel,
        in_specs=[ANY] * 2,
        out_specs=ANY,
        out_shape=piece,
        scratch_shapes=[pltpu.VMEM(piece.shape, bf16), pltpu.SemaphoreType.DMA((2,))],
        compiler_params=vmem(60),
        cost_estimate=cost(0, MIB),
    )(out_weight, partial_value)
    last = lax.ppermute(last_piece, both, across)
    pieces = [mine, by_z, by_x, last]
    pieces = pieces + [lax.ppermute(p, both, other_core) for p in pieces]

    lines = channels * 4 * ctx + 4 * TILE
    flat = (quarters, ctx * channels, lanes)
    held = [
        pltpu.VMEM((3 * (position // 2), position // 2), bf16),
        pltpu.VMEM(flat, f32),
        pltpu.VMEM((channels, 2 * ctx, position), f32),
        pltpu.VMEM((lines, position), bf16),
        pltpu.VMEM((lines, position // 2), f32),
    ]
    spec = pl.pallas_call(
        spectrum_kernel,
        in_specs=[VMEM, ANY],
        out_specs=ANY,
        out_shape=jax.ShapeDtypeStruct((SPARE * lines, position // 2), f32),
        scratch_shapes=[pltpu.VMEM(table.shape, f32), *held, pltpu.SemaphoreType.DMA((2,))],
        compiler_params=vmem(58),
        cost_estimate=cost(4 * 10**9, 4 * MIB),
    )(taps, table)
    mixed = pl.pallas_call(
        conv_kernel,
        in_specs=[SMEM, VMEM, ANY, VMEM],
        out_specs=ANY,
        out_shape=jax.ShapeDtypeStruct((ch, ctx, channels, position), bf16),
        scratch_shapes=[
            pltpu.VMEM((lines, position // 2), f32),
            *held,
            pltpu.VMEM((channels, 4 * ctx, position), bf16),
            pltpu.VMEM(flat, f32),
            pltpu.VMEM((ctx, channels, position), bf16),
            pltpu.SemaphoreType.DMA((1,)),
            pltpu.SemaphoreType.DMA((4,)),
        ],
        compiler_params=vmem(40),
        cost_estimate=cost(8 * 10**9, 6 * MIB),
    )(skip_gain, parts, spec, table)

    mixed = lax.all_to_all(
        mixed.reshape(devices, channels, position),
        ("ch", "ctx"), split_axis=0, concat_axis=0, tiled=True,
    ).reshape(width, position)

    steps = features // 1024
    weights = pl.pallas_call(
        weights_kernel,
        in_specs=[ANY] * (1 + len(pieces)),
        out_specs=ANY,
        out_shape=jax.ShapeDtypeStruct((steps, width, features // steps), bf16),
        scratch_shapes=[
            pltpu.VMEM((width, features), bf16),
            pltpu.SemaphoreType.DMA((1 + len(pieces),)),
            pltpu.SemaphoreType.DMA((steps,)),
        ],
        compiler_params=vmem(60),
        cost_estimate=cost(0, 16 * MIB),
    )(out_weight, *pieces)

    return pl.pallas_call(
        out_kernel,
        in_specs=[VMEM, ANY],
        out_specs=ANY,
        out_shape=jax.ShapeDtypeStruct((position, features), bf16),
        scratch_shapes=[
            pltpu.VMEM((position, width), bf16),
            pltpu.VMEM((steps, width, features // steps), bf16),
            pltpu.VMEM((position, features), bf16),
            pltpu.SemaphoreType.DMA((steps + 1,)),
            pltpu.SemaphoreType.DMA((steps + LAST_PARTS,)),
        ],
        compiler_params=vmem(48),
        cost_estimate=cost(2 * position * features * width, 13 * MIB),
    )(mixed, weights)


def solution(mesh):
    return jax.shard_map(
        shards,
        mesh=mesh,
        in_specs=(P("ctx", "ch"), P("ch", None), P("ctx", "ch"), P("ch"), P("ch", None)),
        out_specs=P("ctx", "ch"),
        check_vma=False,
    )
```

```python
import numpy as np
import ml_dtypes
import jax
import jax.numpy as jnp
from jax import lax
from jax.experimental import pallas as pl
from jax.experimental.pallas import tpu as pltpu
from jax.sharding import PartitionSpec as P

bf16 = jnp.bfloat16
f32 = jnp.float32
MIB = 1024 * 1024
TILE = 16
GROUP = 4
CHUNK = 512
SPARE = 12
LAST_PARTS = 4
PIECES = 4


def split_table(table):
    high = table.astype(ml_dtypes.bfloat16)
    low = (table - high.astype(np.float64)).astype(ml_dtypes.bfloat16)
    return high, low


def tables(blocks, width):
    period = 2 * blocks * width
    quarter = width // 4
    freq = np.arange(blocks)[:, None]
    angle = 2.0 * np.pi * (freq * np.arange(blocks)[None, :] % (2 * blocks)) / (2 * blocks)
    lead_high, lead_low = split_table(np.concatenate([np.cos(angle), -np.sin(angle)], axis=0))
    weight = np.where(freq == 0, 1.0, 2.0) / period
    cosines, sines = np.cos(angle) * weight, np.sin(angle) * weight
    sines[0] = (1.0 - 2.0 * (np.arange(blocks) % 2)) / period
    tail_high, tail_low = split_table(np.concatenate([cosines, sines], axis=0).T)
    turned = np.concatenate([freq, np.full((TILE, 1), blocks)])
    turn = 2.0 * np.pi * turned * np.arange(width)[None, :] / period
    fold = 2.0 * np.pi * np.arange(4)[:, None] * np.arange(quarter)[None, :] / width
    index = np.arange(quarter)
    line = 2.0 * np.pi * (index[:, None] * index[None, :] % quarter) / quarter
    cos, sin = np.cos(line), np.sin(line)
    line_high, line_low = split_table(np.block([[cos, -sin], [sin, cos]]))
    parts = [
        line_high,
        line_low,
        np.concatenate([lead_high, lead_high, lead_low], axis=1),
        np.concatenate([lead_high, lead_low], axis=1),
        np.block([[tail_high, tail_high], [tail_low, np.zeros_like(tail_low)]]),
        *np.split(np.cos(turn), 2, axis=1),
        *np.split(np.sin(turn), 2, axis=1),
        np.concatenate([np.cos(fold), np.sin(fold)]),
    ]
    columns = line_high.shape[1]
    return np.concatenate(
        [np.pad(p.astype(np.float32), ((0, 0), (0, columns - p.shape[1]))) for p in parts]
    )


def unpack(table_ref, blocks, line_ref):
    columns = line_ref.shape[1]
    line_ref[:columns] = table_ref[:columns, :].astype(bf16)
    line_ref[columns:] = table_ref[: 2 * columns, :].astype(bf16)
    at = 2 * columns
    leads = []
    for use in (3 * blocks, 2 * blocks, 4 * blocks):
        leads.append(table_ref[at : at + 2 * blocks, :use].astype(bf16))
        at += 2 * blocks
    rows = blocks + TILE
    quarter = columns // 2

    def twist(first, p):
        lanes = slice(quarter * (p % 2), quarter * (p % 2 + 1))
        start = at + p // 2 * rows + first
        return [table_ref[start + 2 * i * rows : start + 2 * i * rows + TILE, lanes] for i in range(2)]

    end = at + 4 * rows
    return (*leads, table_ref[end : end + 8, :quarter], twist)


def dot(a, b):
    return jnp.dot(a, b, preferred_element_type=f32)


def split(a):
    high = a.astype(bf16)
    return high, (a - high.astype(f32)).astype(bf16)


def turn_back(real, imag, cos, sin):
    return real * cos + imag * sin, imag * cos - real * sin


def butterfly(parts):
    (ar, ai), (br, bi), (cr, ci), (dr, di) = parts
    sr, si, er, ei = ar + cr, ai + ci, ar - cr, ai - ci
    tr, ti, fr, fi = br + dr, bi + di, br - dr, bi - di
    return [(sr + tr, si + ti), (er + fi, ei - fr), (sr - tr, si - ti), (er - fi, ei + fr)]


def put_rows(rows_ref, at, value):
    high, low = split(value)
    size = value.shape[1]
    span = pl.ds(at, value.shape[0])
    rows_ref[span, :size] = high
    rows_ref[span, size : 2 * size] = low


def transform_rows(rows_ref, at, count, line_ref):
    size = line_ref.shape[1]
    span = pl.ds(at, count)
    both = dot(rows_ref[span, :], line_ref[: 2 * size, :])
    return both + dot(rows_ref[span, :size], line_ref[2 * size :, :])


def spread(real, imag, first, rows_ref, at, twist, fold):
    quarter = real.shape[1] // 4
    parts = []
    for p in range(4):
        lanes = slice(quarter * p, quarter * (p + 1))
        cos, sin = twist(first, p)
        if imag is None:
            parts.append((real[:, lanes] * cos, -real[:, lanes] * sin))
        else:
            parts.append(turn_back(real[:, lanes], imag[:, lanes], cos, sin))
    for r, (a, b) in enumerate(butterfly(parts)):
        if r:
            a, b = turn_back(a, b, fold[r : r + 1], fold[r + 4 : r + 5])
        put_rows(rows_ref, at + TILE * r, jnp.concatenate([a, b], axis=1))


def gather_back(back_ref, at, first, twist, fold):
    quarter = back_ref.shape[1] // 2
    got = []
    for r in range(4):
        span = pl.ds(at + TILE * r, TILE)
        a, b = back_ref[span, :quarter], back_ref[span, quarter:]
        if r:
            a, b = turn_back(a, b, fold[r : r + 1], fold[r + 4 : r + 5])
        got.append((a, b))
    reals, imags = [], []
    for p, (a, b) in enumerate(butterfly(got)):
        a, b = turn_back(a, b, *twist(first, p))
        reals.append(a)
        imags.append(b)
    return jnp.concatenate(reals, axis=1), jnp.concatenate(imags, axis=1)


def where():
    here = lax.axis_index("ctx")
    return lax.axis_index("ch"), here & 1, here >> 3 & 3, here >> 1 & 3


def held_pieces(x, z):
    first = (x & 1) * 2 + (z & 1)
    return [first ^ flip for flip in range(PIECES)]


def start_all(pairs, sems):
    copies = [pltpu.make_async_copy(a, b, sems.at[i]) for i, (a, b) in enumerate(pairs)]
    for copy in copies:
        copy.start()
    return copies


def forward(load, last, lead, lines_ref, rows_ref, spec_ref, twist, fold, line_ref):
    channels = lines_ref.shape[0]
    blocks = lines_ref.shape[1] // 2
    tiles = blocks // TILE
    size = blocks * 4
    end = channels * size
    spread(last, None, blocks, rows_ref, end, twist, fold)
    for step in range(channels // GROUP):
        held = range(GROUP * step, GROUP * (step + 1))
        for c in held:
            lines_ref[c] = dot(lead, load(c))
        for c in held:
            for t in range(tiles):
                real = lines_ref[c, pl.ds(TILE * t, TILE), :]
                imag = lines_ref[c, pl.ds(blocks + TILE * t, TILE), :]
                spread(real, imag, TILE * t, rows_ref, c * size + 4 * TILE * t, twist, fold)
        count = GROUP * size + (4 * TILE if step == channels // GROUP - 1 else 0)
        spec_ref[pl.ds(GROUP * size * step, count), :] = transform_rows(
            rows_ref, GROUP * size * step, count, line_ref
        )


def fill(flat, planes):
    blocks, channels, width = planes.shape
    rows = planes.reshape(blocks * channels, width)
    for q in range(width // 128):
        flat[q, : blocks * channels] = rows[:, 128 * q : 128 * (q + 1)]


def channel_of(flat, channel, blocks, channels):
    place = pl.ds(channel, blocks, stride=channels)
    return jnp.concatenate([flat[q, place, :] for q in range(flat.shape[0])], axis=1)


def alternating(planes):
    pairs = planes.reshape(planes.shape[0] // 2, 2, *planes.shape[1:])
    rows = jnp.sum(pairs[:, 0] - pairs[:, 1], axis=0)
    return jnp.concatenate([rows, jnp.zeros((TILE - rows.shape[0], rows.shape[1]), f32)], axis=0)


def spectrum_kernel(
    taps_ref, table_hbm, spec_hbm,
    table_ref, line_ref, flat, lines_ref, rows_ref, spec_ref, sems,
):
    blocks, channels, _ = taps_ref.shape
    copies = start_all([(table_hbm, table_ref)], sems)
    taps = taps_ref[...].astype(f32)
    fill(flat, taps)
    last = alternating(taps)
    for copy in copies:
        copy.wait()

    def load(c):
        value = channel_of(flat, c, blocks, channels).astype(bf16)
        return jnp.concatenate([value, value], axis=0)

    _, lead, _, fold, twist = unpack(table_ref, blocks, line_ref)
    forward(load, last, lead, lines_ref, rows_ref, spec_ref, twist, fold, line_ref)
    copy = pltpu.make_async_copy(spec_ref, spec_hbm.at[pl.ds(0, spec_ref.shape[0])], sems.at[1])
    copy.start()
    copy.wait()


def conv_kernel(
    gain_ref, parts_ref, spec_hbm, table_ref, out_hbm,
    taps_spec_ref, line_ref,
    flat, lines_ref, rows_ref, spec_ref, packed_ref, mixed_ref, out_ref, sems, out_sems,
):
    blocks, _, channels, width = parts_ref.shape
    lanes = flat.shape[2]
    quarters = width // lanes
    quarter = spec_ref.shape[1] // 2
    tiles = blocks // TILE
    size = blocks * 4
    half = blocks // 2
    copies = start_all([(spec_hbm.at[pl.ds(0, taps_spec_ref.shape[0])], taps_spec_ref)], sems)
    total = parts_ref[:, 0].astype(f32) + parts_ref[:, 1].astype(f32)
    fill(flat, total)
    last = alternating(total)
    lead, _, tail, fold, twist = unpack(table_ref, blocks, line_ref)

    def load(c):
        high, low = split(channel_of(flat, c, blocks, channels))
        return jnp.concatenate([high, low, high], axis=0)

    forward(load, last, lead, lines_ref, rows_ref, spec_ref, twist, fold, line_ref)
    copies[0].wait()

    def multiply(at, gain):
        span = pl.ds(at, 4 * TILE)
        real, imag = spec_ref[span, :quarter], spec_ref[span, quarter:]
        taps_real, taps_imag = taps_spec_ref[span, :quarter] + gain, taps_spec_ref[span, quarter:]
        put_rows(
            rows_ref, at,
            jnp.concatenate(
                [real * taps_real - imag * taps_imag, -(real * taps_imag + imag * taps_real)], axis=1
            ),
        )

    first_gain = lax.axis_index("ctx") * channels
    gain = [gain_ref[first_gain + c] for c in range(channels)]
    end = channels * size
    row = lax.broadcasted_iota(jnp.int32, (4 * TILE, quarter), 0) % TILE
    all_gains = jnp.zeros((4 * TILE, quarter), f32)
    for c in range(channels):
        all_gains = jnp.where(row == c, gain[c], all_gains)
    multiply(end, all_gains)
    spec_ref[pl.ds(end, 4 * TILE), :] = transform_rows(rows_ref, end, 4 * TILE, line_ref)
    last, _ = gather_back(spec_ref, end, blocks, twist, fold)
    first_row = lax.broadcasted_iota(jnp.int32, (TILE, width), 0) == 0
    for step in range(channels // GROUP):
        held = range(GROUP * step, GROUP * (step + 1))
        for c in held:
            for t in range(tiles):
                multiply(c * size + 4 * TILE * t, gain[c])
        at = GROUP * size * step
        spec_ref[pl.ds(at, GROUP * size), :] = transform_rows(rows_ref, at, GROUP * size, line_ref)
        for c in held:
            for t in range(tiles):
                real, imag = gather_back(spec_ref, c * size + 4 * TILE * t, TILE * t, twist, fold)
                if t == 0:
                    imag = jnp.where(first_row, last[c : c + 1], imag)
                for at, part in ((TILE * t, real), (blocks + TILE * t, imag)):
                    high, low = split(part)
                    packed_ref[c, pl.ds(at, TILE), :] = high
                    packed_ref[c, pl.ds(2 * blocks + at, TILE), :] = low
    for c in range(channels):
        both = dot(tail, packed_ref[c])
        value = both[:blocks] + both[blocks:]
        for q in range(quarters):
            mixed_ref[q, pl.ds(c, blocks, stride=channels), :] = value[:, lanes * q : lanes * (q + 1)]
    stores = []
    for i in range(2):
        span = pl.ds(half * i, half)
        for q in range(quarters):
            result = mixed_ref[q, pl.ds(half * channels * i, half * channels), :].astype(bf16)
            out_ref[span, :, lanes * q : lanes * (q + 1)] = result.reshape(half, channels, lanes)
        for k in range(2):
            stores.append(
                pltpu.make_async_copy(out_ref.at[span], out_hbm.at[span, k], out_sems.at[2 * i + k])
            )
            stores[-1].start()
    for copy in stores:
        copy.wait()


def prepare_kernel(
    taps_hbm, weight_hbm, out_hbm, piece_hbm, taps_ref, out_ref, piece_ref, sems, out_sems
):
    steps = sems.shape[0] - 1
    size = taps_ref.shape[0] // steps
    spans = [pl.ds(i * size, size) for i in range(steps)]
    loads = start_all(
        [(taps_hbm.at[s], taps_ref.at[s]) for s in spans]
        + [(piece_source(weight_hbm, piece_hbm, 0), piece_ref)],
        sems,
    )
    for load in loads[:steps]:
        load.wait()
    stores = []
    for i, span in enumerate(spans):
        out_ref[span, :] = taps_ref[:, i * size : (i + 1) * size].astype(bf16).T
        stores.append(pltpu.make_async_copy(out_ref.at[span], out_hbm.at[span], out_sems.at[i]))
        stores[-1].start()
    loads[steps].wait()
    stores.append(pltpu.make_async_copy(piece_ref, piece_hbm, out_sems.at[steps]))
    stores[-1].start()
    for store in stores:
        store.wait()


def piece_source(weight_hbm, piece_ref, chosen):
    group, core, x, z = where()
    size, columns = piece_ref.shape
    at = pl.ds(pl.multiple_of((1 - group) * columns, columns), columns)
    start = (core * PIECES + held_pieces(x, z)[chosen]) * size
    return weight_hbm.at[pl.ds(pl.multiple_of(start, size), size), at]


def last_piece_kernel(weight_hbm, after_ref, out_hbm, piece_ref, sems):
    source = piece_source(weight_hbm, out_hbm, PIECES - 1)
    for a, b, sem in ((source, piece_ref, sems.at[0]), (piece_ref, out_hbm, sems.at[1])):
        copy = pltpu.make_async_copy(a, b, sem)
        copy.start()
        copy.wait()


def fence_kernel(value_ref, after_ref, out_ref):
    pass


def project_kernel(
    tokens_hbm, weight_hbm, out_hbm, tokens_ref, weight_ref, total, out_ref,
    token_sems, weight_sems, out_sems,
):
    features = tokens_ref.shape[1]
    width = weight_ref.shape[1]
    ctx, ch, channels, _ = out_hbm.shape
    steps = features // CHUNK
    parts = 4
    loads = []
    for i in range(steps):
        at = pl.ds(i * CHUNK, CHUNK)
        pair = (
            pltpu.make_async_copy(tokens_hbm.at[:, at], tokens_ref.at[:, at], token_sems.at[i]),
            pltpu.make_async_copy(weight_hbm.at[at], weight_ref.at[at], weight_sems.at[i]),
        )
        for copy in pair:
            copy.start()
        loads.append(pair)
    stores = []
    for i in range(steps):
        for copy in loads[i]:
            copy.wait()
        at = slice(i * CHUNK, (i + 1) * CHUNK)
        for c in range(parts):
            cols = slice(c * width // parts, (c + 1) * width // parts)
            term = dot(tokens_ref[:, at], weight_ref[at, cols])
            if i == 0:
                total[:, cols] = term
            elif i < steps - 1:
                total[:, cols] += term
            else:
                turned = (total[:, cols] + term).astype(bf16).T
                count = ctx * ch // parts
                span = pl.ds(c * count, count)
                out_ref[span] = turned.reshape(count, channels, turned.shape[1])
                place = out_hbm.at[pl.ds(c * count % ctx, count), c * count // ctx]
                store = pltpu.make_async_copy(out_ref.at[span], place, out_sems.at[c])
                store.start()
                stores.append(store)
    for store in stores:
        store.wait()


def weights_kernel(own_hbm, *rest):
    pieces, (out_hbm, held_ref, sems, out_sems) = rest[:-4], rest[-4:]
    rows = own_hbm.shape[0]
    blocks, _, columns = out_hbm.shape
    group = where()[0]
    at = pl.ds(pl.multiple_of(group * (blocks * columns), columns), blocks * columns)
    pairs = [(own_hbm.at[:, at], held_ref.at[pl.ds(0, rows)])]
    for piece in pieces:
        size = piece.shape[0]
        pairs.append((piece, held_ref.at[pl.ds(rows, size)]))
        rows += size
    for copy in start_all(pairs, sems):
        copy.wait()
    stores = start_all(
        [(held_ref.at[:, pl.ds(b * columns, columns)], out_hbm.at[b]) for b in range(blocks)],
        out_sems,
    )
    for copy in stores:
        copy.wait()


def out_kernel(mixed_ref, weight_hbm, out_hbm, turned, weight_ref, out_ref, sems, out_sems):
    steps, _, columns = weight_ref.shape
    ctx, _, channels, position = mixed_ref.shape
    rows = ctx * channels
    parts = [(0, pl.ds(0, rows)), (0, pl.ds(rows, rows)), *range(1, steps)]
    loads = start_all([(weight_hbm.at[i], weight_ref.at[i]) for i in parts], sems)
    group, core, x, z = where()
    size = ctx // (2 * PIECES)
    turned[:, :rows] = mixed_ref[:, group].reshape(rows, position).T
    pieces = []
    for half in (core, 1 - core):
        for k in held_pieces(x, z):
            start = (half * PIECES + k) * size
            pieces.append(mixed_ref[pl.ds(start, size), 1 - group])
    turned[:, rows:] = jnp.concatenate(pieces, axis=0).reshape(rows, position).T
    loads[0].wait()
    own_part = dot(turned[:, :rows], weight_ref[0, :rows])
    loads[1].wait()
    out_ref[:, :columns] = (own_part + dot(turned[:, rows:], weight_ref[0, rows:])).astype(bf16)
    stores = []
    for i in range(1, steps):
        loads[i + 1].wait()
        at = slice(i * columns, (i + 1) * columns)
        if i < steps - 1:
            out_ref[:, at] = dot(turned[...], weight_ref[i]).astype(bf16)
            if i % 2:
                stores.append((slice(None), pl.ds((i - 1) * columns, 2 * columns)))
            elif i == steps - 2:
                stores.append((slice(None), pl.ds(i * columns, columns)))
            else:
                continue
            start_store(out_ref, out_hbm, out_sems, stores)
            continue
        count = turned.shape[0] // LAST_PARTS
        for r in range(LAST_PARTS):
            part = slice(r * count, (r + 1) * count)
            out_ref[part, at] = dot(turned[part, :], weight_ref[i]).astype(bf16)
            stores.append((pl.ds(r * count, count), pl.ds(i * columns, columns)))
            start_store(out_ref, out_hbm, out_sems, stores)
    for i, span in enumerate(stores):
        pltpu.make_async_copy(out_ref.at[span], out_hbm.at[span], out_sems.at[i]).wait()


def start_store(out_ref, out_hbm, out_sems, stores):
    span = stores[-1]
    pltpu.make_async_copy(out_ref.at[span], out_hbm.at[span], out_sems.at[len(stores) - 1]).start()


def vmem(limit):
    return pltpu.CompilerParams(vmem_limit_bytes=limit * MIB)


def cost(flops, size):
    return pl.CostEstimate(flops=flops, bytes_accessed=size, transcendentals=0)


ANY = pl.BlockSpec(memory_space=pl.ANY)
SMEM = pl.BlockSpec(memory_space=pltpu.SMEM)
VMEM = pl.BlockSpec(memory_space=pltpu.VMEM)


def partners(move):
    def place(y, x, z, core):
        return (((y % 2 * 4 + x) * 4 + z) * 2 + core) * 2 + y // 2

    spots = [(y, x, z, c) for y in range(4) for x in range(4) for z in range(4) for c in range(2)]
    return [(place(*spot), place(*move(*spot))) for spot in spots]


def shards(tokens, in_weight, filter_taps, skip_gain, out_weight):
    ctx, ch = lax.axis_size("ctx"), lax.axis_size("ch")
    devices = ctx * ch
    position, features = tokens.shape
    width = in_weight.shape[1]
    channels = width // devices
    rows = out_weight.shape[0]
    table = jnp.asarray(tables(ctx, position))
    lanes = 128
    quarters = position // lanes
    both = ("ctx", "ch")
    across = partners(lambda y, x, z, c: (3 - y, x, z, c))
    other_core = partners(lambda y, x, z, c: (y, x, z, 1 - c))
    along_x = partners(lambda y, x, z, c: (y, x ^ 1, z, c))
    along_z = partners(lambda y, x, z, c: (y, x, z ^ 1, c))
    size = rows // (2 * PIECES)

    piece = jax.ShapeDtypeStruct((size, features), bf16)
    taps, first_piece = pl.pallas_call(
        prepare_kernel,
        in_specs=[ANY] * 2,
        out_specs=[ANY] * 2,
        out_shape=[jax.ShapeDtypeStruct((width // ch, position), bf16), piece],
        scratch_shapes=[
            pltpu.VMEM((position, width // ch), f32),
            pltpu.VMEM((width // ch, position), bf16),
            pltpu.VMEM(piece.shape, bf16),
            pltpu.SemaphoreType.DMA((5,)),
            pltpu.SemaphoreType.DMA((5,)),
        ],
        compiler_params=vmem(60),
        cost_estimate=cost(0, 2 * MIB),
    )(filter_taps, out_weight)
    mine = lax.ppermute(first_piece, both, across)
    taps = lax.all_to_all(
        taps.reshape(ctx, channels, position), "ctx", split_axis=0, concat_axis=0, tiled=True
    )

    partial_value = pl.pallas_call(
        project_kernel,
        in_specs=[ANY] * 2,
        out_specs=ANY,
        out_shape=jax.ShapeDtypeStruct((ctx, ch, channels, position), bf16),
        scratch_shapes=[
            pltpu.VMEM((position, features), bf16),
            pltpu.VMEM((features, width), bf16),
            pltpu.VMEM((position, width), f32),
            pltpu.VMEM((devices, channels, position), bf16),
            pltpu.SemaphoreType.DMA((features // CHUNK,)),
            pltpu.SemaphoreType.DMA((features // CHUNK,)),
            pltpu.SemaphoreType.DMA((4,)),
        ],
        compiler_params=vmem(60),
        cost_estimate=cost(2 * position * features * width, 14 * MIB),
    )(tokens, in_weight)
    partial_value = pl.pallas_call(
        fence_kernel,
        in_specs=[ANY] * 2,
        out_specs=ANY,
        out_shape=jax.ShapeDtypeStruct(partial_value.shape, bf16),
        input_output_aliases={0: 0},
        compiler_params=vmem(60),
        cost_estimate=cost(0, 0),
    )(partial_value, mine)
    parts = lax.all_to_all(
        partial_value.reshape(devices, channels, position),
        both, split_axis=0, concat_axis=0, tiled=True,
    ).reshape(ctx, ch, channels, position)

    by_x = lax.ppermute(mine, both, along_x)
    by_z = lax.ppermute(mine, both, along_z)
    last_piece = pl.pallas_call(
        last_piece_kernel,
        in_specs=[ANY] * 2,
        out_specs=ANY,
        out_shape=piece,
        scratch_shapes=[pltpu.VMEM(piece.shape, bf16), pltpu.SemaphoreType.DMA((2,))],
        compiler_params=vmem(60),
        cost_estimate=cost(0, MIB),
    )(out_weight, partial_value)
    last = lax.ppermute(last_piece, both, across)
    pieces = [mine, by_z, by_x, last]
    pieces = pieces + [lax.ppermute(p, both, other_core) for p in pieces]

    lines = channels * 4 * ctx + 4 * TILE
    flat = (quarters, ctx * channels, lanes)
    held = [
        pltpu.VMEM((3 * (position // 2), position // 2), bf16),
        pltpu.VMEM(flat, f32),
        pltpu.VMEM((channels, 2 * ctx, position), f32),
        pltpu.VMEM((lines, position), bf16),
        pltpu.VMEM((lines, position // 2), f32),
    ]
    spec = pl.pallas_call(
        spectrum_kernel,
        in_specs=[VMEM, ANY],
        out_specs=ANY,
        out_shape=jax.ShapeDtypeStruct((SPARE * lines, position // 2), f32),
        scratch_shapes=[pltpu.VMEM(table.shape, f32), *held, pltpu.SemaphoreType.DMA((2,))],
        compiler_params=vmem(58),
        cost_estimate=cost(4 * 10**9, 4 * MIB),
    )(taps, table)
    mixed = pl.pallas_call(
        conv_kernel,
        in_specs=[SMEM, VMEM, ANY, VMEM],
        out_specs=ANY,
        out_shape=jax.ShapeDtypeStruct((ctx, ch, channels, position), bf16),
        scratch_shapes=[
            pltpu.VMEM((lines, position // 2), f32),
            *held,
            pltpu.VMEM((channels, 4 * ctx, position), bf16),
            pltpu.VMEM(flat, f32),
            pltpu.VMEM((ctx, channels, position), bf16),
            pltpu.SemaphoreType.DMA((1,)),
            pltpu.SemaphoreType.DMA((4,)),
        ],
        compiler_params=vmem(40),
        cost_estimate=cost(8 * 10**9, 6 * MIB),
    )(skip_gain, parts, spec, table)

    mixed = lax.all_to_all(
        mixed.reshape(devices, channels, position),
        both, split_axis=0, concat_axis=0, tiled=True,
    ).reshape(ctx, ch, channels, position)

    steps = features // 1024
    weights = pl.pallas_call(
        weights_kernel,
        in_specs=[ANY] * (1 + len(pieces)),
        out_specs=ANY,
        out_shape=jax.ShapeDtypeStruct((steps, width, features // steps), bf16),
        scratch_shapes=[
            pltpu.VMEM((width, features), bf16),
            pltpu.SemaphoreType.DMA((1 + len(pieces),)),
            pltpu.SemaphoreType.DMA((steps,)),
        ],
        compiler_params=vmem(60),
        cost_estimate=cost(0, 16 * MIB),
    )(out_weight, *pieces)

    return pl.pallas_call(
        out_kernel,
        in_specs=[VMEM, ANY],
        out_specs=ANY,
        out_shape=jax.ShapeDtypeStruct((position, features), bf16),
        scratch_shapes=[
            pltpu.VMEM((position, width), bf16),
            pltpu.VMEM((steps, width, features // steps), bf16),
            pltpu.VMEM((position, features), bf16),
            pltpu.SemaphoreType.DMA((steps + 1,)),
            pltpu.SemaphoreType.DMA((steps + LAST_PARTS,)),
        ],
        compiler_params=vmem(48),
        cost_estimate=cost(2 * position * features * width, 13 * MIB),
    )(mixed, weights)


def solution(mesh):
    return jax.shard_map(
        shards,
        mesh=mesh,
        in_specs=(P("ctx", "ch"), P("ch", None), P("ctx", "ch"), P("ch"), P("ch", None)),
        out_specs=P("ctx", "ch"),
        check_vma=False,
    )
```

```python
import numpy as np
import ml_dtypes
import jax
import jax.numpy as jnp
from jax import lax
from jax.experimental import pallas as pl
from jax.experimental.pallas import tpu as pltpu
from jax.sharding import PartitionSpec as P

bf16 = jnp.bfloat16
f32 = jnp.float32
MIB = 1024 * 1024
TILE = 16
GROUP = 4
CHUNK = 512
SPARE = 12
LAST_PARTS = 4
PIECES = 4


def split_table(table):
    high = table.astype(ml_dtypes.bfloat16)
    low = (table - high.astype(np.float64)).astype(ml_dtypes.bfloat16)
    return high, low


def tables(blocks, width):
    period = 2 * blocks * width
    quarter = width // 4
    freq = np.arange(blocks)[:, None]
    angle = 2.0 * np.pi * (freq * np.arange(blocks)[None, :] % (2 * blocks)) / (2 * blocks)
    lead_high, lead_low = split_table(np.concatenate([np.cos(angle), -np.sin(angle)], axis=0))
    weight = np.where(freq == 0, 1.0, 2.0) / period
    cosines, sines = np.cos(angle) * weight, np.sin(angle) * weight
    sines[0] = (1.0 - 2.0 * (np.arange(blocks) % 2)) / period
    tail_high, tail_low = split_table(np.concatenate([cosines, sines], axis=0).T)
    turned = np.concatenate([freq, np.full((TILE, 1), blocks)])
    turn = 2.0 * np.pi * turned * np.arange(width)[None, :] / period
    fold = 2.0 * np.pi * np.arange(4)[:, None] * np.arange(quarter)[None, :] / width
    index = np.arange(quarter)
    line = 2.0 * np.pi * (index[:, None] * index[None, :] % quarter) / quarter
    cos, sin = np.cos(line), np.sin(line)
    line_high, line_low = split_table(np.block([[cos, -sin], [sin, cos]]))
    parts = [
        line_high,
        line_low,
        np.concatenate([lead_high, lead_high, lead_low], axis=1),
        np.concatenate([lead_high, lead_low], axis=1),
        np.block([[tail_high, tail_high], [tail_low, np.zeros_like(tail_low)]]),
        *np.split(np.cos(turn), 2, axis=1),
        *np.split(np.sin(turn), 2, axis=1),
        np.concatenate([np.cos(fold), np.sin(fold)]),
    ]
    columns = line_high.shape[1]
    return np.concatenate(
        [np.pad(p.astype(np.float32), ((0, 0), (0, columns - p.shape[1]))) for p in parts]
    )


def unpack(table_ref, blocks, line_ref):
    columns = line_ref.shape[1]
    line_ref[:columns] = table_ref[:columns, :].astype(bf16)
    line_ref[columns:] = table_ref[: 2 * columns, :].astype(bf16)
    at = 2 * columns
    leads = []
    for use in (3 * blocks, 2 * blocks, 4 * blocks):
        leads.append(table_ref[at : at + 2 * blocks, :use].astype(bf16))
        at += 2 * blocks
    rows = blocks + TILE
    quarter = columns // 2

    def twist(first, p):
        lanes = slice(quarter * (p % 2), quarter * (p % 2 + 1))
        start = at + p // 2 * rows + first
        return [table_ref[start + 2 * i * rows : start + 2 * i * rows + TILE, lanes] for i in range(2)]

    end = at + 4 * rows
    return (*leads, table_ref[end : end + 8, :quarter], twist)


def dot(a, b):
    return jnp.dot(a, b, preferred_element_type=f32)


def split(a):
    high = a.astype(bf16)
    return high, (a - high.astype(f32)).astype(bf16)


def turn_back(real, imag, cos, sin):
    return real * cos + imag * sin, imag * cos - real * sin


def butterfly(parts):
    (ar, ai), (br, bi), (cr, ci), (dr, di) = parts
    sr, si, er, ei = ar + cr, ai + ci, ar - cr, ai - ci
    tr, ti, fr, fi = br + dr, bi + di, br - dr, bi - di
    return [(sr + tr, si + ti), (er + fi, ei - fr), (sr - tr, si - ti), (er - fi, ei + fr)]


def put_rows(rows_ref, at, value):
    high, low = split(value)
    size = value.shape[1]
    span = pl.ds(at, value.shape[0])
    rows_ref[span, :size] = high
    rows_ref[span, size : 2 * size] = low


def transform_rows(rows_ref, at, count, line_ref):
    size = line_ref.shape[1]
    span = pl.ds(at, count)
    both = dot(rows_ref[span, :], line_ref[: 2 * size, :])
    return both + dot(rows_ref[span, :size], line_ref[2 * size :, :])


def spread(real, imag, first, rows_ref, at, twist, fold):
    quarter = real.shape[1] // 4
    parts = []
    for p in range(4):
        lanes = slice(quarter * p, quarter * (p + 1))
        cos, sin = twist(first, p)
        if imag is None:
            parts.append((real[:, lanes] * cos, -real[:, lanes] * sin))
        else:
            parts.append(turn_back(real[:, lanes], imag[:, lanes], cos, sin))
    for r, (a, b) in enumerate(butterfly(parts)):
        if r:
            a, b = turn_back(a, b, fold[r : r + 1], fold[r + 4 : r + 5])
        put_rows(rows_ref, at + TILE * r, jnp.concatenate([a, b], axis=1))


def gather_back(back_ref, at, first, twist, fold):
    quarter = back_ref.shape[1] // 2
    got = []
    for r in range(4):
        span = pl.ds(at + TILE * r, TILE)
        a, b = back_ref[span, :quarter], back_ref[span, quarter:]
        if r:
            a, b = turn_back(a, b, fold[r : r + 1], fold[r + 4 : r + 5])
        got.append((a, b))
    reals, imags = [], []
    for p, (a, b) in enumerate(butterfly(got)):
        a, b = turn_back(a, b, *twist(first, p))
        reals.append(a)
        imags.append(b)
    return jnp.concatenate(reals, axis=1), jnp.concatenate(imags, axis=1)


def where():
    here = lax.axis_index("ctx")
    return lax.axis_index("ch"), here & 1, here >> 3 & 3, here >> 1 & 3


def held_pieces(x, z):
    first = (x & 1) * 2 + (z & 1)
    return [first ^ flip for flip in range(PIECES)]


def start_all(pairs, sems):
    copies = [pltpu.make_async_copy(a, b, sems.at[i]) for i, (a, b) in enumerate(pairs)]
    for copy in copies:
        copy.start()
    return copies


def forward(load, last, lead, lines_ref, rows_ref, spec_ref, twist, fold, line_ref):
    channels = lines_ref.shape[0]
    blocks = lines_ref.shape[1] // 2
    tiles = blocks // TILE
    size = blocks * 4
    end = channels * size
    spread(last, None, blocks, rows_ref, end, twist, fold)
    for step in range(channels // GROUP):
        held = range(GROUP * step, GROUP * (step + 1))
        for c in held:
            lines_ref[c] = dot(lead, load(c))
        for c in held:
            for t in range(tiles):
                real = lines_ref[c, pl.ds(TILE * t, TILE), :]
                imag = lines_ref[c, pl.ds(blocks + TILE * t, TILE), :]
                spread(real, imag, TILE * t, rows_ref, c * size + 4 * TILE * t, twist, fold)
        count = GROUP * size + (4 * TILE if step == channels // GROUP - 1 else 0)
        spec_ref[pl.ds(GROUP * size * step, count), :] = transform_rows(
            rows_ref, GROUP * size * step, count, line_ref
        )


def fill(flat, planes):
    blocks, channels, width = planes.shape
    rows = planes.reshape(blocks * channels, width)
    for q in range(width // 128):
        flat[q, : blocks * channels] = rows[:, 128 * q : 128 * (q + 1)]


def channel_of(flat, channel, blocks, channels):
    place = pl.ds(channel, blocks, stride=channels)
    return jnp.concatenate([flat[q, place, :] for q in range(flat.shape[0])], axis=1)


def alternating(planes):
    pairs = planes.reshape(planes.shape[0] // 2, 2, *planes.shape[1:])
    rows = jnp.sum(pairs[:, 0] - pairs[:, 1], axis=0)
    return jnp.concatenate([rows, jnp.zeros((TILE - rows.shape[0], rows.shape[1]), f32)], axis=0)


def spectrum_kernel(
    taps_ref, table_hbm, spec_hbm,
    table_ref, line_ref, flat, lines_ref, rows_ref, spec_ref, sems,
):
    blocks, channels, _ = taps_ref.shape
    copies = start_all([(table_hbm, table_ref)], sems)
    taps = taps_ref[...].astype(f32)
    fill(flat, taps)
    last = alternating(taps)
    for copy in copies:
        copy.wait()

    def load(c):
        value = channel_of(flat, c, blocks, channels).astype(bf16)
        return jnp.concatenate([value, value], axis=0)

    _, lead, _, fold, twist = unpack(table_ref, blocks, line_ref)
    forward(load, last, lead, lines_ref, rows_ref, spec_ref, twist, fold, line_ref)
    copy = pltpu.make_async_copy(spec_ref, spec_hbm.at[pl.ds(0, spec_ref.shape[0])], sems.at[1])
    copy.start()
    copy.wait()


def conv_kernel(
    gain_ref, parts_ref, spec_hbm, table_ref, out_hbm,
    taps_spec_ref, line_ref,
    flat, lines_ref, rows_ref, spec_ref, packed_ref, mixed_ref, out_ref, sems, out_sems,
):
    blocks, _, channels, width = parts_ref.shape
    lanes = flat.shape[2]
    quarters = width // lanes
    quarter = spec_ref.shape[1] // 2
    tiles = blocks // TILE
    size = blocks * 4
    half = blocks // 2
    copies = start_all([(spec_hbm.at[pl.ds(0, taps_spec_ref.shape[0])], taps_spec_ref)], sems)
    total = parts_ref[:, 0].astype(f32) + parts_ref[:, 1].astype(f32)
    fill(flat, total)
    last = alternating(total)
    lead, _, tail, fold, twist = unpack(table_ref, blocks, line_ref)

    def load(c):
        high, low = split(channel_of(flat, c, blocks, channels))
        return jnp.concatenate([high, low, high], axis=0)

    forward(load, last, lead, lines_ref, rows_ref, spec_ref, twist, fold, line_ref)
    copies[0].wait()

    def multiply(at, gain):
        span = pl.ds(at, 4 * TILE)
        real, imag = spec_ref[span, :quarter], spec_ref[span, quarter:]
        taps_real, taps_imag = taps_spec_ref[span, :quarter] + gain, taps_spec_ref[span, quarter:]
        put_rows(
            rows_ref, at,
            jnp.concatenate(
                [real * taps_real - imag * taps_imag, -(real * taps_imag + imag * taps_real)], axis=1
            ),
        )

    first_gain = lax.axis_index("ctx") * channels
    gain = [gain_ref[first_gain + c] for c in range(channels)]
    end = channels * size
    row = lax.broadcasted_iota(jnp.int32, (4 * TILE, quarter), 0) % TILE
    all_gains = jnp.zeros((4 * TILE, quarter), f32)
    for c in range(channels):
        all_gains = jnp.where(row == c, gain[c], all_gains)
    multiply(end, all_gains)
    spec_ref[pl.ds(end, 4 * TILE), :] = transform_rows(rows_ref, end, 4 * TILE, line_ref)
    last, _ = gather_back(spec_ref, end, blocks, twist, fold)
    first_row = lax.broadcasted_iota(jnp.int32, (TILE, width), 0) == 0
    for step in range(channels // GROUP):
        held = range(GROUP * step, GROUP * (step + 1))
        for c in held:
            for t in range(tiles):
                multiply(c * size + 4 * TILE * t, gain[c])
        at = GROUP * size * step
        spec_ref[pl.ds(at, GROUP * size), :] = transform_rows(rows_ref, at, GROUP * size, line_ref)
        for c in held:
            for t in range(tiles):
                real, imag = gather_back(spec_ref, c * size + 4 * TILE * t, TILE * t, twist, fold)
                if t == 0:
                    imag = jnp.where(first_row, last[c : c + 1], imag)
                for at, part in ((TILE * t, real), (blocks + TILE * t, imag)):
                    high, low = split(part)
                    packed_ref[c, pl.ds(at, TILE), :] = high
                    packed_ref[c, pl.ds(2 * blocks + at, TILE), :] = low
    for c in range(channels):
        both = dot(tail, packed_ref[c])
        value = both[:blocks] + both[blocks:]
        for q in range(quarters):
            mixed_ref[q, pl.ds(c, blocks, stride=channels), :] = value[:, lanes * q : lanes * (q + 1)]
    stores = []
    for i in range(2):
        span = pl.ds(half * i, half)
        for q in range(quarters):
            result = mixed_ref[q, pl.ds(half * channels * i, half * channels), :].astype(bf16)
            out_ref[span, :, lanes * q : lanes * (q + 1)] = result.reshape(half, channels, lanes)
        for k in range(2):
            stores.append(
                pltpu.make_async_copy(out_ref.at[span], out_hbm.at[span, k], out_sems.at[2 * i + k])
            )
            stores[-1].start()
    for copy in stores:
        copy.wait()


def prepare_kernel(
    taps_hbm, weight_hbm, out_hbm, piece_hbm, taps_ref, out_ref, piece_ref, sems, out_sems
):
    steps = sems.shape[0] - 1
    size = taps_ref.shape[1] // steps
    spans = [pl.ds(i * size, size) for i in range(steps)]
    loads = start_all(
        [(taps_hbm.at[:, s], taps_ref.at[:, s]) for s in spans]
        + [(piece_source(weight_hbm, piece_hbm, 0), piece_ref)],
        sems,
    )
    stores = []
    for i in range(steps):
        loads[i].wait()
        at = slice(i * size, (i + 1) * size)
        out_ref[at, :] = taps_ref[:, at].astype(bf16).T
        stores.append(pltpu.make_async_copy(out_ref.at[spans[i]], out_hbm.at[spans[i]], out_sems.at[i]))
        stores[-1].start()
    loads[steps].wait()
    stores.append(pltpu.make_async_copy(piece_ref, piece_hbm, out_sems.at[steps]))
    stores[-1].start()
    for store in stores:
        store.wait()


def piece_source(weight_hbm, piece_ref, chosen):
    group, core, x, z = where()
    size, columns = piece_ref.shape
    at = pl.ds(pl.multiple_of((1 - group) * columns, columns), columns)
    start = (core * PIECES + held_pieces(x, z)[chosen]) * size
    return weight_hbm.at[pl.ds(pl.multiple_of(start, size), size), at]


def last_piece_kernel(weight_hbm, after_ref, out_hbm, piece_ref, sems):
    source = piece_source(weight_hbm, out_hbm, PIECES - 1)
    for a, b, sem in ((source, piece_ref, sems.at[0]), (piece_ref, out_hbm, sems.at[1])):
        copy = pltpu.make_async_copy(a, b, sem)
        copy.start()
        copy.wait()


def fence_kernel(value_ref, after_ref, out_ref):
    pass


def project_kernel(
    tokens_hbm, weight_hbm, out_hbm, tokens_ref, weight_ref, total, out_ref,
    token_sems, weight_sems, out_sems,
):
    features = tokens_ref.shape[1]
    width = weight_ref.shape[1]
    ctx, ch, channels, _ = out_hbm.shape
    steps = features // CHUNK
    parts = 4
    loads = []
    for i in range(steps):
        at = pl.ds(i * CHUNK, CHUNK)
        pair = (
            pltpu.make_async_copy(tokens_hbm.at[:, at], tokens_ref.at[:, at], token_sems.at[i]),
            pltpu.make_async_copy(weight_hbm.at[at], weight_ref.at[at], weight_sems.at[i]),
        )
        for copy in pair:
            copy.start()
        loads.append(pair)
    stores = []
    for i in range(steps):
        for copy in loads[i]:
            copy.wait()
        at = slice(i * CHUNK, (i + 1) * CHUNK)
        for c in range(parts):
            cols = slice(c * width // parts, (c + 1) * width // parts)
            term = dot(tokens_ref[:, at], weight_ref[at, cols])
            if i == 0:
                total[:, cols] = term
            elif i < steps - 1:
                total[:, cols] += term
            else:
                turned = (total[:, cols] + term).astype(bf16).T
                count = ctx * ch // parts
                span = pl.ds(c * count, count)
                out_ref[span] = turned.reshape(count, channels, turned.shape[1])
                place = out_hbm.at[pl.ds(c * count % ctx, count), c * count // ctx]
                store = pltpu.make_async_copy(out_ref.at[span], place, out_sems.at[c])
                store.start()
                stores.append(store)
    for store in stores:
        store.wait()


def weights_kernel(own_hbm, *rest):
    pieces, (out_hbm, held_ref, sems, out_sems) = rest[:-4], rest[-4:]
    rows = own_hbm.shape[0]
    blocks, _, columns = out_hbm.shape
    group = where()[0]
    at = pl.ds(pl.multiple_of(group * (blocks * columns), columns), blocks * columns)
    pairs = [(own_hbm.at[:, at], held_ref.at[pl.ds(0, rows)])]
    for piece in pieces:
        size = piece.shape[0]
        pairs.append((piece, held_ref.at[pl.ds(rows, size)]))
        rows += size
    for copy in start_all(pairs, sems):
        copy.wait()
    stores = start_all(
        [(held_ref.at[:, pl.ds(b * columns, columns)], out_hbm.at[b]) for b in range(blocks)],
        out_sems,
    )
    for copy in stores:
        copy.wait()


def out_kernel(mixed_ref, weight_hbm, out_hbm, turned, weight_ref, out_ref, sems, out_sems):
    steps, _, columns = weight_ref.shape
    ctx, _, channels, position = mixed_ref.shape
    rows = ctx * channels
    parts = [(0, pl.ds(0, rows)), (0, pl.ds(rows, rows)), *range(1, steps)]
    loads = start_all([(weight_hbm.at[i], weight_ref.at[i]) for i in parts], sems)
    group, core, x, z = where()
    size = ctx // (2 * PIECES)
    turned[:, :rows] = mixed_ref[:, group].reshape(rows, position).T
    loads[0].wait()
    own_part = dot(turned[:, :rows], weight_ref[0, :rows])
    pieces = []
    for half in (core, 1 - core):
        for k in held_pieces(x, z):
            start = (half * PIECES + k) * size
            pieces.append(mixed_ref[pl.ds(start, size), 1 - group])
    turned[:, rows:] = jnp.concatenate(pieces, axis=0).reshape(rows, position).T
    loads[1].wait()
    out_ref[:, :columns] = (own_part + dot(turned[:, rows:], weight_ref[0, rows:])).astype(bf16)
    stores = []
    for i in range(1, steps):
        loads[i + 1].wait()
        at = slice(i * columns, (i + 1) * columns)
        if i < steps - 1:
            out_ref[:, at] = dot(turned[...], weight_ref[i]).astype(bf16)
            if i % 2:
                stores.append((slice(None), pl.ds((i - 1) * columns, 2 * columns)))
            elif i == steps - 2:
                stores.append((slice(None), pl.ds(i * columns, columns)))
            else:
                continue
            start_store(out_ref, out_hbm, out_sems, stores)
            continue
        count = turned.shape[0] // LAST_PARTS
        for r in range(LAST_PARTS):
            part = slice(r * count, (r + 1) * count)
            out_ref[part, at] = dot(turned[part, :], weight_ref[i]).astype(bf16)
            stores.append((pl.ds(r * count, count), pl.ds(i * columns, columns)))
            start_store(out_ref, out_hbm, out_sems, stores)
    for i, span in enumerate(stores):
        pltpu.make_async_copy(out_ref.at[span], out_hbm.at[span], out_sems.at[i]).wait()


def start_store(out_ref, out_hbm, out_sems, stores):
    span = stores[-1]
    pltpu.make_async_copy(out_ref.at[span], out_hbm.at[span], out_sems.at[len(stores) - 1]).start()


def vmem(limit):
    return pltpu.CompilerParams(vmem_limit_bytes=limit * MIB)


def cost(flops, size):
    return pl.CostEstimate(flops=flops, bytes_accessed=size, transcendentals=0)


ANY = pl.BlockSpec(memory_space=pl.ANY)
SMEM = pl.BlockSpec(memory_space=pltpu.SMEM)
VMEM = pl.BlockSpec(memory_space=pltpu.VMEM)


def partners(move):
    def place(y, x, z, core):
        return (((y % 2 * 4 + x) * 4 + z) * 2 + core) * 2 + y // 2

    spots = [(y, x, z, c) for y in range(4) for x in range(4) for z in range(4) for c in range(2)]
    return [(place(*spot), place(*move(*spot))) for spot in spots]


def shards(tokens, in_weight, filter_taps, skip_gain, out_weight):
    ctx, ch = lax.axis_size("ctx"), lax.axis_size("ch")
    devices = ctx * ch
    position, features = tokens.shape
    width = in_weight.shape[1]
    channels = width // devices
    rows = out_weight.shape[0]
    table = jnp.asarray(tables(ctx, position))
    lanes = 128
    quarters = position // lanes
    both = ("ctx", "ch")
    across = partners(lambda y, x, z, c: (3 - y, x, z, c))
    other_core = partners(lambda y, x, z, c: (y, x, z, 1 - c))
    along_x = partners(lambda y, x, z, c: (y, x ^ 1, z, c))
    along_z = partners(lambda y, x, z, c: (y, x, z ^ 1, c))
    size = rows // (2 * PIECES)

    piece = jax.ShapeDtypeStruct((size, features), bf16)
    taps, first_piece = pl.pallas_call(
        prepare_kernel,
        in_specs=[ANY] * 2,
        out_specs=[ANY] * 2,
        out_shape=[jax.ShapeDtypeStruct((width // ch, position), bf16), piece],
        scratch_shapes=[
            pltpu.VMEM((position, width // ch), f32),
            pltpu.VMEM((width // ch, position), bf16),
            pltpu.VMEM(piece.shape, bf16),
            pltpu.SemaphoreType.DMA((3,)),
            pltpu.SemaphoreType.DMA((3,)),
        ],
        compiler_params=vmem(60),
        cost_estimate=cost(0, 2 * MIB),
    )(filter_taps, out_weight)
    mine = lax.ppermute(first_piece, both, across)
    taps = lax.all_to_all(
        taps.reshape(ctx, channels, position), "ctx", split_axis=0, concat_axis=0, tiled=True
    )

    partial_value = pl.pallas_call(
        project_kernel,
        in_specs=[ANY] * 2,
        out_specs=ANY,
        out_shape=jax.ShapeDtypeStruct((ctx, ch, channels, position), bf16),
        scratch_shapes=[
            pltpu.VMEM((position, features), bf16),
            pltpu.VMEM((features, width), bf16),
            pltpu.VMEM((position, width), f32),
            pltpu.VMEM((devices, channels, position), bf16),
            pltpu.SemaphoreType.DMA((features // CHUNK,)),
            pltpu.SemaphoreType.DMA((features // CHUNK,)),
            pltpu.SemaphoreType.DMA((4,)),
        ],
        compiler_params=vmem(60),
        cost_estimate=cost(2 * position * features * width, 14 * MIB),
    )(tokens, in_weight)
    partial_value = pl.pallas_call(
        fence_kernel,
        in_specs=[ANY] * 2,
        out_specs=ANY,
        out_shape=jax.ShapeDtypeStruct(partial_value.shape, bf16),
        input_output_aliases={0: 0},
        compiler_params=vmem(60),
        cost_estimate=cost(0, 0),
    )(partial_value, mine)
    parts = lax.all_to_all(
        partial_value.reshape(devices, channels, position),
        both, split_axis=0, concat_axis=0, tiled=True,
    ).reshape(ctx, ch, channels, position)

    by_x = lax.ppermute(mine, both, along_x)
    by_z = lax.ppermute(mine, both, along_z)
    last_piece = pl.pallas_call(
        last_piece_kernel,
        in_specs=[ANY] * 2,
        out_specs=ANY,
        out_shape=piece,
        scratch_shapes=[pltpu.VMEM(piece.shape, bf16), pltpu.SemaphoreType.DMA((2,))],
        compiler_params=vmem(60),
        cost_estimate=cost(0, MIB),
    )(out_weight, partial_value)
    last = lax.ppermute(last_piece, both, across)
    pieces = [mine, by_z, by_x, last]
    pieces = pieces + [lax.ppermute(p, both, other_core) for p in pieces]

    lines = channels * 4 * ctx + 4 * TILE
    flat = (quarters, ctx * channels, lanes)
    held = [
        pltpu.VMEM((3 * (position // 2), position // 2), bf16),
        pltpu.VMEM(flat, f32),
        pltpu.VMEM((channels, 2 * ctx, position), f32),
        pltpu.VMEM((lines, position), bf16),
        pltpu.VMEM((lines, position // 2), f32),
    ]
    spec = pl.pallas_call(
        spectrum_kernel,
        in_specs=[VMEM, ANY],
        out_specs=ANY,
        out_shape=jax.ShapeDtypeStruct((SPARE * lines, position // 2), f32),
        scratch_shapes=[pltpu.VMEM(table.shape, f32), *held, pltpu.SemaphoreType.DMA((2,))],
        compiler_params=vmem(58),
        cost_estimate=cost(4 * 10**9, 4 * MIB),
    )(taps, table)
    mixed = pl.pallas_call(
        conv_kernel,
        in_specs=[SMEM, VMEM, ANY, VMEM],
        out_specs=ANY,
        out_shape=jax.ShapeDtypeStruct((ctx, ch, channels, position), bf16),
        scratch_shapes=[
            pltpu.VMEM((lines, position // 2), f32),
            *held,
            pltpu.VMEM((channels, 4 * ctx, position), bf16),
            pltpu.VMEM(flat, f32),
            pltpu.VMEM((ctx, channels, position), bf16),
            pltpu.SemaphoreType.DMA((1,)),
            pltpu.SemaphoreType.DMA((4,)),
        ],
        compiler_params=vmem(40),
        cost_estimate=cost(8 * 10**9, 6 * MIB),
    )(skip_gain, parts, spec, table)

    mixed = lax.all_to_all(
        mixed.reshape(devices, channels, position),
        both, split_axis=0, concat_axis=0, tiled=True,
    ).reshape(ctx, ch, channels, position)

    steps = features // 1024
    weights = pl.pallas_call(
        weights_kernel,
        in_specs=[ANY] * (1 + len(pieces)),
        out_specs=ANY,
        out_shape=jax.ShapeDtypeStruct((steps, width, features // steps), bf16),
        scratch_shapes=[
            pltpu.VMEM((width, features), bf16),
            pltpu.SemaphoreType.DMA((1 + len(pieces),)),
            pltpu.SemaphoreType.DMA((steps,)),
        ],
        compiler_params=vmem(60),
        cost_estimate=cost(0, 16 * MIB),
    )(out_weight, *pieces)

    return pl.pallas_call(
        out_kernel,
        in_specs=[VMEM, ANY],
        out_specs=ANY,
        out_shape=jax.ShapeDtypeStruct((position, features), bf16),
        scratch_shapes=[
            pltpu.VMEM((position, width), bf16),
            pltpu.VMEM((steps, width, features // steps), bf16),
            pltpu.VMEM((position, features), bf16),
            pltpu.SemaphoreType.DMA((steps + 1,)),
            pltpu.SemaphoreType.DMA((steps + LAST_PARTS,)),
        ],
        compiler_params=vmem(48),
        cost_estimate=cost(2 * position * features * width, 13 * MIB),
    )(mixed, weights)


def solution(mesh):
    return jax.shard_map(
        shards,
        mesh=mesh,
        in_specs=(P("ctx", "ch"), P("ch", None), P("ctx", "ch"), P("ch"), P("ch", None)),
        out_specs=P("ctx", "ch"),
        check_vma=False,
    )
```

```python
import numpy as np
import ml_dtypes
import jax
import jax.numpy as jnp
from jax import lax
from jax.experimental import pallas as pl
from jax.experimental.pallas import tpu as pltpu
from jax.sharding import PartitionSpec as P

bf16 = jnp.bfloat16
f32 = jnp.float32
MIB = 1024 * 1024
TILE = 16
GROUP = 4
CHUNK = 512
SPARE = 12
LAST_PARTS = 4
PIECES = 4


def split_table(table):
    high = table.astype(ml_dtypes.bfloat16)
    low = (table - high.astype(np.float64)).astype(ml_dtypes.bfloat16)
    return high, low


def tables(blocks, width):
    period = 2 * blocks * width
    quarter = width // 4
    freq = np.arange(blocks)[:, None]
    angle = 2.0 * np.pi * (freq * np.arange(blocks)[None, :] % (2 * blocks)) / (2 * blocks)
    lead_high, lead_low = split_table(np.concatenate([np.cos(angle), -np.sin(angle)], axis=0))
    weight = np.where(freq == 0, 1.0, 2.0) / period
    cosines, sines = np.cos(angle) * weight, np.sin(angle) * weight
    sines[0] = (1.0 - 2.0 * (np.arange(blocks) % 2)) / period
    tail_high, tail_low = split_table(np.concatenate([cosines, sines], axis=0).T)
    turned = np.concatenate([freq, np.full((TILE, 1), blocks)])
    turn = 2.0 * np.pi * turned * np.arange(width)[None, :] / period
    fold = 2.0 * np.pi * np.arange(4)[:, None] * np.arange(quarter)[None, :] / width
    index = np.arange(quarter)
    line = 2.0 * np.pi * (index[:, None] * index[None, :] % quarter) / quarter
    cos, sin = np.cos(line), np.sin(line)
    line_high, line_low = split_table(np.block([[cos, -sin], [sin, cos]]))
    parts = [
        line_high,
        line_low,
        np.concatenate([lead_high, lead_high, lead_low], axis=1),
        np.concatenate([lead_high, lead_low], axis=1),
        np.block([[tail_high, tail_high], [tail_low, np.zeros_like(tail_low)]]),
        *np.split(np.cos(turn), 2, axis=1),
        *np.split(np.sin(turn), 2, axis=1),
        np.concatenate([np.cos(fold), np.sin(fold)]),
    ]
    columns = line_high.shape[1]
    return np.concatenate(
        [np.pad(p.astype(np.float32), ((0, 0), (0, columns - p.shape[1]))) for p in parts]
    )


def unpack(table_ref, blocks, line_ref):
    columns = line_ref.shape[1]
    line_ref[:columns] = table_ref[:columns, :].astype(bf16)
    line_ref[columns:] = table_ref[: 2 * columns, :].astype(bf16)
    at = 2 * columns
    leads = []
    for use in (3 * blocks, 2 * blocks, 4 * blocks):
        leads.append(table_ref[at : at + 2 * blocks, :use].astype(bf16))
        at += 2 * blocks
    rows = blocks + TILE
    quarter = columns // 2

    def twist(first, p):
        lanes = slice(quarter * (p % 2), quarter * (p % 2 + 1))
        start = at + p // 2 * rows + first
        return [table_ref[start + 2 * i * rows : start + 2 * i * rows + TILE, lanes] for i in range(2)]

    end = at + 4 * rows
    return (*leads, table_ref[end : end + 8, :quarter], twist)


def dot(a, b):
    return jnp.dot(a, b, preferred_element_type=f32)


def split(a):
    high = a.astype(bf16)
    return high, (a - high.astype(f32)).astype(bf16)


def turn_back(real, imag, cos, sin):
    return real * cos + imag * sin, imag * cos - real * sin


def butterfly(parts):
    (ar, ai), (br, bi), (cr, ci), (dr, di) = parts
    sr, si, er, ei = ar + cr, ai + ci, ar - cr, ai - ci
    tr, ti, fr, fi = br + dr, bi + di, br - dr, bi - di
    return [(sr + tr, si + ti), (er + fi, ei - fr), (sr - tr, si - ti), (er - fi, ei + fr)]


def put_rows(rows_ref, at, value):
    high, low = split(value)
    size = value.shape[1]
    span = pl.ds(at, value.shape[0])
    rows_ref[span, :size] = high
    rows_ref[span, size : 2 * size] = low


def transform_rows(rows_ref, at, count, line_ref):
    size = line_ref.shape[1]
    span = pl.ds(at, count)
    both = dot(rows_ref[span, :], line_ref[: 2 * size, :])
    return both + dot(rows_ref[span, :size], line_ref[2 * size :, :])


def spread(real, imag, first, rows_ref, at, twist, fold):
    quarter = real.shape[1] // 4
    parts = []
    for p in range(4):
        lanes = slice(quarter * p, quarter * (p + 1))
        cos, sin = twist(first, p)
        if imag is None:
            parts.append((real[:, lanes] * cos, -real[:, lanes] * sin))
        else:
            parts.append(turn_back(real[:, lanes], imag[:, lanes], cos, sin))
    for r, (a, b) in enumerate(butterfly(parts)):
        if r:
            a, b = turn_back(a, b, fold[r : r + 1], fold[r + 4 : r + 5])
        put_rows(rows_ref, at + TILE * r, jnp.concatenate([a, b], axis=1))


def gather_back(back_ref, at, first, twist, fold):
    quarter = back_ref.shape[1] // 2
    got = []
    for r in range(4):
        span = pl.ds(at + TILE * r, TILE)
        a, b = back_ref[span, :quarter], back_ref[span, quarter:]
        if r:
            a, b = turn_back(a, b, fold[r : r + 1], fold[r + 4 : r + 5])
        got.append((a, b))
    reals, imags = [], []
    for p, (a, b) in enumerate(butterfly(got)):
        a, b = turn_back(a, b, *twist(first, p))
        reals.append(a)
        imags.append(b)
    return jnp.concatenate(reals, axis=1), jnp.concatenate(imags, axis=1)


def where():
    here = lax.axis_index("ctx")
    return lax.axis_index("ch"), here & 1, here >> 3 & 3, here >> 1 & 3


def held_pieces(x, z):
    first = (x & 1) * 2 + (z & 1)
    return [first ^ flip for flip in range(PIECES)]


def start_all(pairs, sems):
    copies = [pltpu.make_async_copy(a, b, sems.at[i]) for i, (a, b) in enumerate(pairs)]
    for copy in copies:
        copy.start()
    return copies


def forward(load, last, lead, lines_ref, rows_ref, spec_ref, twist, fold, line_ref):
    channels = lines_ref.shape[0]
    blocks = lines_ref.shape[1] // 2
    tiles = blocks // TILE
    size = blocks * 4
    end = channels * size
    spread(last, None, blocks, rows_ref, end, twist, fold)
    for step in range(channels // GROUP):
        held = range(GROUP * step, GROUP * (step + 1))
        for c in held:
            lines_ref[c] = dot(lead, load(c))
        for c in held:
            for t in range(tiles):
                real = lines_ref[c, pl.ds(TILE * t, TILE), :]
                imag = lines_ref[c, pl.ds(blocks + TILE * t, TILE), :]
                spread(real, imag, TILE * t, rows_ref, c * size + 4 * TILE * t, twist, fold)
        count = GROUP * size + (4 * TILE if step == channels // GROUP - 1 else 0)
        spec_ref[pl.ds(GROUP * size * step, count), :] = transform_rows(
            rows_ref, GROUP * size * step, count, line_ref
        )


def fill(flat, planes):
    blocks, channels, width = planes.shape
    rows = planes.reshape(blocks * channels, width)
    for q in range(width // 128):
        flat[q, : blocks * channels] = rows[:, 128 * q : 128 * (q + 1)]


def channel_of(flat, channel, blocks, channels):
    place = pl.ds(channel, blocks, stride=channels)
    return jnp.concatenate([flat[q, place, :] for q in range(flat.shape[0])], axis=1)


def alternating(planes):
    pairs = planes.reshape(planes.shape[0] // 2, 2, *planes.shape[1:])
    rows = jnp.sum(pairs[:, 0] - pairs[:, 1], axis=0)
    return jnp.concatenate([rows, jnp.zeros((TILE - rows.shape[0], rows.shape[1]), f32)], axis=0)


def spectrum_kernel(
    taps_ref, table_hbm, spec_hbm,
    table_ref, line_ref, flat, lines_ref, rows_ref, spec_ref, sems,
):
    blocks, channels, _ = taps_ref.shape
    copies = start_all([(table_hbm, table_ref)], sems)
    taps = taps_ref[...].astype(f32)
    fill(flat, taps)
    last = alternating(taps)
    for copy in copies:
        copy.wait()

    def load(c):
        value = channel_of(flat, c, blocks, channels).astype(bf16)
        return jnp.concatenate([value, value], axis=0)

    _, lead, _, fold, twist = unpack(table_ref, blocks, line_ref)
    forward(load, last, lead, lines_ref, rows_ref, spec_ref, twist, fold, line_ref)
    copy = pltpu.make_async_copy(spec_ref, spec_hbm.at[pl.ds(0, spec_ref.shape[0])], sems.at[1])
    copy.start()
    copy.wait()


def conv_kernel(
    gain_ref, parts_ref, spec_hbm, table_ref, out_hbm,
    taps_spec_ref, line_ref,
    flat, lines_ref, rows_ref, spec_ref, packed_ref, mixed_ref, out_ref, sems, out_sems,
):
    blocks, _, channels, width = parts_ref.shape
    lanes = flat.shape[2]
    quarters = width // lanes
    quarter = spec_ref.shape[1] // 2
    tiles = blocks // TILE
    size = blocks * 4
    half = blocks // 2
    copies = start_all([(spec_hbm.at[pl.ds(0, taps_spec_ref.shape[0])], taps_spec_ref)], sems)
    total = parts_ref[:, 0].astype(f32) + parts_ref[:, 1].astype(f32)
    fill(flat, total)
    last = alternating(total)
    lead, _, tail, fold, twist = unpack(table_ref, blocks, line_ref)

    def load(c):
        high, low = split(channel_of(flat, c, blocks, channels))
        return jnp.concatenate([high, low, high], axis=0)

    forward(load, last, lead, lines_ref, rows_ref, spec_ref, twist, fold, line_ref)
    copies[0].wait()

    def multiply(at, gain):
        span = pl.ds(at, 4 * TILE)
        real, imag = spec_ref[span, :quarter], spec_ref[span, quarter:]
        taps_real, taps_imag = taps_spec_ref[span, :quarter] + gain, taps_spec_ref[span, quarter:]
        put_rows(
            rows_ref, at,
            jnp.concatenate(
                [real * taps_real - imag * taps_imag, -(real * taps_imag + imag * taps_real)], axis=1
            ),
        )

    first_gain = lax.axis_index("ctx") * channels
    gain = [gain_ref[first_gain + c] for c in range(channels)]
    end = channels * size
    row = lax.broadcasted_iota(jnp.int32, (4 * TILE, quarter), 0) % TILE
    all_gains = jnp.zeros((4 * TILE, quarter), f32)
    for c in range(channels):
        all_gains = jnp.where(row == c, gain[c], all_gains)
    multiply(end, all_gains)
    spec_ref[pl.ds(end, 4 * TILE), :] = transform_rows(rows_ref, end, 4 * TILE, line_ref)
    last, _ = gather_back(spec_ref, end, blocks, twist, fold)
    first_row = lax.broadcasted_iota(jnp.int32, (TILE, width), 0) == 0
    for step in range(channels // GROUP):
        held = range(GROUP * step, GROUP * (step + 1))
        for c in held:
            for t in range(tiles):
                multiply(c * size + 4 * TILE * t, gain[c])
        at = GROUP * size * step
        spec_ref[pl.ds(at, GROUP * size), :] = transform_rows(rows_ref, at, GROUP * size, line_ref)
        for c in held:
            for t in range(tiles):
                real, imag = gather_back(spec_ref, c * size + 4 * TILE * t, TILE * t, twist, fold)
                if t == 0:
                    imag = jnp.where(first_row, last[c : c + 1], imag)
                for at, part in ((TILE * t, real), (blocks + TILE * t, imag)):
                    high, low = split(part)
                    packed_ref[c, pl.ds(at, TILE), :] = high
                    packed_ref[c, pl.ds(2 * blocks + at, TILE), :] = low
    for c in range(channels):
        both = dot(tail, packed_ref[c])
        value = both[:blocks] + both[blocks:]
        for q in range(quarters):
            mixed_ref[q, pl.ds(c, blocks, stride=channels), :] = value[:, lanes * q : lanes * (q + 1)]
    stores = []
    for i in range(2):
        span = pl.ds(half * i, half)
        for q in range(quarters):
            result = mixed_ref[q, pl.ds(half * channels * i, half * channels), :].astype(bf16)
            out_ref[span, :, lanes * q : lanes * (q + 1)] = result.reshape(half, channels, lanes)
        for k in range(2):
            stores.append(
                pltpu.make_async_copy(out_ref.at[span], out_hbm.at[span, k], out_sems.at[2 * i + k])
            )
            stores[-1].start()
    for copy in stores:
        copy.wait()


def prepare_kernel(
    taps_hbm, weight_hbm, out_hbm, piece_hbm, taps_ref, out_ref, piece_ref, sems, out_sems
):
    steps = sems.shape[0] - 1
    size = taps_ref.shape[1] // steps
    spans = [pl.ds(i * size, size) for i in range(steps)]
    loads = start_all(
        [(taps_hbm.at[:, s], taps_ref.at[:, s]) for s in spans]
        + [(piece_source(weight_hbm, piece_hbm, 0), piece_ref)],
        sems,
    )
    stores = []
    for i in range(steps):
        loads[i].wait()
        at = slice(i * size, (i + 1) * size)
        out_ref[at, :] = taps_ref[:, at].astype(bf16).T
        stores.append(pltpu.make_async_copy(out_ref.at[spans[i]], out_hbm.at[spans[i]], out_sems.at[i]))
        stores[-1].start()
    loads[steps].wait()
    stores.append(pltpu.make_async_copy(piece_ref, piece_hbm, out_sems.at[steps]))
    stores[-1].start()
    for store in stores:
        store.wait()


def piece_source(weight_hbm, piece_ref, chosen):
    group, core, x, z = where()
    size, columns = piece_ref.shape
    at = pl.ds(pl.multiple_of((1 - group) * columns, columns), columns)
    start = (core * PIECES + held_pieces(x, z)[chosen]) * size
    return weight_hbm.at[pl.ds(pl.multiple_of(start, size), size), at]


def last_piece_kernel(weight_hbm, after_ref, out_hbm, piece_ref, sems):
    source = piece_source(weight_hbm, out_hbm, PIECES - 1)
    for a, b, sem in ((source, piece_ref, sems.at[0]), (piece_ref, out_hbm, sems.at[1])):
        copy = pltpu.make_async_copy(a, b, sem)
        copy.start()
        copy.wait()


def fence_kernel(value_ref, after_ref, out_ref):
    pass


def project_kernel(
    tokens_hbm, weight_hbm, out_hbm, tokens_ref, weight_ref, total, out_ref,
    token_sems, weight_sems, out_sems,
):
    features = tokens_ref.shape[1]
    width = weight_ref.shape[1]
    ctx, ch, channels, _ = out_hbm.shape
    steps = features // CHUNK
    parts = 4
    loads = []
    for i in range(steps):
        at = pl.ds(i * CHUNK, CHUNK)
        pair = (
            pltpu.make_async_copy(tokens_hbm.at[:, at], tokens_ref.at[:, at], token_sems.at[i]),
            pltpu.make_async_copy(weight_hbm.at[at], weight_ref.at[at], weight_sems.at[i]),
        )
        for copy in pair:
            copy.start()
        loads.append(pair)
    stores = []
    for i in range(steps):
        for copy in loads[i]:
            copy.wait()
        at = slice(i * CHUNK, (i + 1) * CHUNK)
        for c in range(parts):
            cols = slice(c * width // parts, (c + 1) * width // parts)
            term = dot(tokens_ref[:, at], weight_ref[at, cols])
            if i == 0:
                total[:, cols] = term
            elif i < steps - 1:
                total[:, cols] += term
            else:
                turned = (total[:, cols] + term).astype(bf16).T
                count = ctx * ch // parts
                span = pl.ds(c * count, count)
                out_ref[span] = turned.reshape(count, channels, turned.shape[1])
                place = out_hbm.at[pl.ds(c * count % ctx, count), c * count // ctx]
                store = pltpu.make_async_copy(out_ref.at[span], place, out_sems.at[c])
                store.start()
                stores.append(store)
    for store in stores:
        store.wait()


def weights_kernel(own_hbm, *rest):
    pieces, (out_hbm, held_ref, sems, out_sems) = rest[:-4], rest[-4:]
    rows = own_hbm.shape[0]
    blocks, _, columns = out_hbm.shape
    group = where()[0]
    at = pl.ds(pl.multiple_of(group * (blocks * columns), columns), blocks * columns)
    pairs = [(own_hbm.at[:, at], held_ref.at[pl.ds(0, rows)])]
    for piece in pieces:
        size = piece.shape[0]
        pairs.append((piece, held_ref.at[pl.ds(rows, size)]))
        rows += size
    for copy in start_all(pairs, sems):
        copy.wait()
    stores = start_all(
        [(held_ref.at[:, pl.ds(b * columns, columns)], out_hbm.at[b]) for b in range(blocks)],
        out_sems,
    )
    for copy in stores:
        copy.wait()


def out_kernel(mixed_ref, weight_hbm, out_hbm, turned, weight_ref, out_ref, sems, out_sems):
    steps, _, columns = weight_ref.shape
    ctx, _, channels, position = mixed_ref.shape
    rows = ctx * channels
    parts = [(0, pl.ds(0, rows)), (0, pl.ds(rows, rows)), *range(1, steps)]
    loads = start_all([(weight_hbm.at[i], weight_ref.at[i]) for i in parts], sems)
    group, core, x, z = where()
    size = ctx // (2 * PIECES)
    turned[:, :rows] = mixed_ref[:, group].reshape(rows, position).T
    loads[0].wait()
    own_part = dot(turned[:, :rows], weight_ref[0, :rows])
    pieces = []
    for half in (core, 1 - core):
        for k in held_pieces(x, z):
            start = (half * PIECES + k) * size
            pieces.append(mixed_ref[pl.ds(start, size), 1 - group])
    turned[:, rows:] = jnp.concatenate(pieces, axis=0).reshape(rows, position).T
    loads[1].wait()
    out_ref[:, :columns] = (own_part + dot(turned[:, rows:], weight_ref[0, rows:])).astype(bf16)
    stores = []
    for i in range(1, steps):
        loads[i + 1].wait()
        at = slice(i * columns, (i + 1) * columns)
        if i < steps - 1:
            out_ref[:, at] = dot(turned[...], weight_ref[i]).astype(bf16)
            if i % 2:
                stores.append((slice(None), pl.ds((i - 1) * columns, 2 * columns)))
            elif i == steps - 2:
                stores.append((slice(None), pl.ds(i * columns, columns)))
            else:
                continue
            start_store(out_ref, out_hbm, out_sems, stores)
            continue
        count = turned.shape[0] // LAST_PARTS
        for r in range(LAST_PARTS):
            part = slice(r * count, (r + 1) * count)
            out_ref[part, at] = dot(turned[part, :], weight_ref[i]).astype(bf16)
            stores.append((pl.ds(r * count, count), pl.ds(i * columns, columns)))
            start_store(out_ref, out_hbm, out_sems, stores)
    for i, span in enumerate(stores):
        pltpu.make_async_copy(out_ref.at[span], out_hbm.at[span], out_sems.at[i]).wait()


def start_store(out_ref, out_hbm, out_sems, stores):
    span = stores[-1]
    pltpu.make_async_copy(out_ref.at[span], out_hbm.at[span], out_sems.at[len(stores) - 1]).start()


def vmem(limit):
    return pltpu.CompilerParams(vmem_limit_bytes=limit * MIB)


def cost(flops, size):
    return pl.CostEstimate(flops=flops, bytes_accessed=size, transcendentals=0)


ANY = pl.BlockSpec(memory_space=pl.ANY)
SMEM = pl.BlockSpec(memory_space=pltpu.SMEM)
VMEM = pl.BlockSpec(memory_space=pltpu.VMEM)


def partners(move):
    def place(y, x, z, core):
        return (((y % 2 * 4 + x) * 4 + z) * 2 + core) * 2 + y // 2

    spots = [(y, x, z, c) for y in range(4) for x in range(4) for z in range(4) for c in range(2)]
    return [(place(*spot), place(*move(*spot))) for spot in spots]


def shards(tokens, in_weight, filter_taps, skip_gain, out_weight):
    ctx, ch = lax.axis_size("ctx"), lax.axis_size("ch")
    devices = ctx * ch
    position, features = tokens.shape
    width = in_weight.shape[1]
    channels = width // devices
    rows = out_weight.shape[0]
    table = jnp.asarray(tables(ctx, position))
    lanes = 128
    quarters = position // lanes
    both = ("ctx", "ch")
    across = partners(lambda y, x, z, c: (3 - y, x, z, c))
    other_core = partners(lambda y, x, z, c: (y, x, z, 1 - c))
    along_x = partners(lambda y, x, z, c: (y, x ^ 1, z, c))
    along_z = partners(lambda y, x, z, c: (y, x, z ^ 1, c))
    size = rows // (2 * PIECES)

    piece = jax.ShapeDtypeStruct((size, features), bf16)
    taps, first_piece = pl.pallas_call(
        prepare_kernel,
        in_specs=[ANY] * 2,
        out_specs=[ANY] * 2,
        out_shape=[jax.ShapeDtypeStruct((width // ch, position), bf16), piece],
        scratch_shapes=[
            pltpu.VMEM((position, width // ch), f32),
            pltpu.VMEM((width // ch, position), bf16),
            pltpu.VMEM(piece.shape, bf16),
            pltpu.SemaphoreType.DMA((3,)),
            pltpu.SemaphoreType.DMA((3,)),
        ],
        compiler_params=vmem(60),
        cost_estimate=cost(0, 2 * MIB),
    )(filter_taps, out_weight)
    mine = lax.ppermute(first_piece, both, across)
    taps = lax.all_to_all(
        taps.reshape(ctx, channels, position), "ctx", split_axis=0, concat_axis=0, tiled=True
    )

    partial_value = pl.pallas_call(
        project_kernel,
        in_specs=[ANY] * 2,
        out_specs=ANY,
        out_shape=jax.ShapeDtypeStruct((ctx, ch, channels, position), bf16),
        scratch_shapes=[
            pltpu.VMEM((position, features), bf16),
            pltpu.VMEM((features, width), bf16),
            pltpu.VMEM((position, width), f32),
            pltpu.VMEM((devices, channels, position), bf16),
            pltpu.SemaphoreType.DMA((features // CHUNK,)),
            pltpu.SemaphoreType.DMA((features // CHUNK,)),
            pltpu.SemaphoreType.DMA((4,)),
        ],
        compiler_params=vmem(60),
        cost_estimate=cost(2 * position * features * width, 14 * MIB),
    )(tokens, in_weight)
    partial_value = pl.pallas_call(
        fence_kernel,
        in_specs=[ANY] * 2,
        out_specs=ANY,
        out_shape=jax.ShapeDtypeStruct(partial_value.shape, bf16),
        input_output_aliases={0: 0},
        compiler_params=vmem(60),
        cost_estimate=cost(0, 0),
    )(partial_value, mine)
    parts = lax.all_to_all(
        partial_value.reshape(devices, channels, position),
        both, split_axis=0, concat_axis=0, tiled=True,
    ).reshape(ctx, ch, channels, position)

    by_x = lax.ppermute(mine, both, along_x)
    by_z = lax.ppermute(mine, both, along_z)
    last_piece = pl.pallas_call(
        last_piece_kernel,
        in_specs=[ANY] * 2,
        out_specs=ANY,
        out_shape=piece,
        scratch_shapes=[pltpu.VMEM(piece.shape, bf16), pltpu.SemaphoreType.DMA((2,))],
        compiler_params=vmem(60),
        cost_estimate=cost(0, MIB),
    )(out_weight, partial_value)
    last = lax.ppermute(last_piece, both, across)
    pieces = [mine, by_z, by_x, last]
    pieces = pieces + [lax.ppermute(p, both, other_core) for p in pieces]

    lines = channels * 4 * ctx + 4 * TILE
    flat = (quarters, ctx * channels + channels, lanes)
    held = [
        pltpu.VMEM((3 * (position // 2), position // 2), bf16),
        pltpu.VMEM(flat, f32),
        pltpu.VMEM((channels, 2 * ctx, position), f32),
        pltpu.VMEM((lines, position), bf16),
        pltpu.VMEM((lines, position // 2), f32),
    ]
    spec = pl.pallas_call(
        spectrum_kernel,
        in_specs=[VMEM, ANY],
        out_specs=ANY,
        out_shape=jax.ShapeDtypeStruct((SPARE * lines, position // 2), f32),
        scratch_shapes=[pltpu.VMEM(table.shape, f32), *held, pltpu.SemaphoreType.DMA((2,))],
        compiler_params=vmem(58),
        cost_estimate=cost(4 * 10**9, 4 * MIB),
    )(taps, table)
    mixed = pl.pallas_call(
        conv_kernel,
        in_specs=[SMEM, VMEM, ANY, VMEM],
        out_specs=ANY,
        out_shape=jax.ShapeDtypeStruct((ctx, ch, channels, position), bf16),
        scratch_shapes=[
            pltpu.VMEM((lines, position // 2), f32),
            *held,
            pltpu.VMEM((channels, 4 * ctx, position), bf16),
            pltpu.VMEM(flat, f32),
            pltpu.VMEM((ctx, channels, position), bf16),
            pltpu.SemaphoreType.DMA((1,)),
            pltpu.SemaphoreType.DMA((4,)),
        ],
        compiler_params=vmem(40),
        cost_estimate=cost(8 * 10**9, 6 * MIB),
    )(skip_gain, parts, spec, table)

    mixed = lax.all_to_all(
        mixed.reshape(devices, channels, position),
        both, split_axis=0, concat_axis=0, tiled=True,
    ).reshape(ctx, ch, channels, position)

    steps = features // 1024
    weights = pl.pallas_call(
        weights_kernel,
        in_specs=[ANY] * (1 + len(pieces)),
        out_specs=ANY,
        out_shape=jax.ShapeDtypeStruct((steps, width, features // steps), bf16),
        scratch_shapes=[
            pltpu.VMEM((width, features), bf16),
            pltpu.SemaphoreType.DMA((1 + len(pieces),)),
            pltpu.SemaphoreType.DMA((steps,)),
        ],
        compiler_params=vmem(60),
        cost_estimate=cost(0, 16 * MIB),
    )(out_weight, *pieces)

    return pl.pallas_call(
        out_kernel,
        in_specs=[VMEM, ANY],
        out_specs=ANY,
        out_shape=jax.ShapeDtypeStruct((position, features), bf16),
        scratch_shapes=[
            pltpu.VMEM((position, width), bf16),
            pltpu.VMEM((steps, width, features // steps), bf16),
            pltpu.VMEM((position, features), bf16),
            pltpu.SemaphoreType.DMA((steps + 1,)),
            pltpu.SemaphoreType.DMA((steps + LAST_PARTS,)),
        ],
        compiler_params=vmem(48),
        cost_estimate=cost(2 * position * features * width, 13 * MIB),
    )(mixed, weights)


def solution(mesh):
    return jax.shard_map(
        shards,
        mesh=mesh,
        in_specs=(P("ctx", "ch"), P("ch", None), P("ctx", "ch"), P("ch"), P("ch", None)),
        out_specs=P("ctx", "ch"),
        check_vma=False,
    )
```
